512 devices in a mesh: wide: 128 (over y, z, core), narrow: 4 (over x).
Axes of the slice: x: 4, y: 4, z: 16, core: 2. Of those that a mesh axis runs over, the one named last changes fastest.
Arguments:
- mobility: float32 [2048, 64, 256], P('wide', 'narrow'), may hold values from 0.2 to 5
- sav_vector: float32 [2048, 64, 256], P('wide', 'narrow'), may hold values from -8 to 8
- cotangent: float32 [2048, 64, 256], P('wide', 'narrow'), may hold values from -8 to 8
Outputs:
- adjoint: float32 [2048, 64, 256], P('wide', 'narrow')
The draws below stay inside these ranges and needn't reach their ends.
All inputs are finite; a program needn't handle non-finite values.
Results may differ from the reference program's by a relative error of at most 0.0019.
Values sent between devices are 32-bit elements; how exact they have to be, the bound alone decides.
No kernel may reach another device: no remote copies, remote signals or barrier semaphores. Data moves between devices by JAX's collectives and lax.ppermute only.
A program may use at most 128 MiB of HBM per device.

```python
import math
import jax
import jax.numpy as jnp

NZ = 256
LEVELS = 5
NX = 2048
NY = 64


def shared_part(key):
    return jax.random.normal(jax.random.fold_in(key, 7), (NX, NY, NZ), jnp.float32)


def draw_sav_vector(key, part):
    own_part = jax.random.normal(jax.random.fold_in(key, 11), (NX, NY, NZ), jnp.float32)
    return jnp.clip(shared_part(key) + 0.7 * own_part, -8.0, 8.0)


def draw_cotangent(key, part):
    own_part = jax.random.normal(jax.random.fold_in(key, 13), (NX, NY, NZ), jnp.float32)
    return jnp.clip(shared_part(key) + 0.7 * own_part, -8.0, 8.0)


def level_of(rng, dims, split, least, high):
    gain = 1.0
    for dim, blocks in split:
        steps = jax.random.uniform(jax.random.fold_in(jax.random.fold_in(rng, 6), dim), (blocks,), jnp.float32, least / len(split), high / len(split))
        gain = gain * jnp.repeat(jnp.exp(steps), dims[dim] // blocks).reshape((-1,) + (1,) * (len(dims) - 1 - dim))
    return gain


def setup_inputs(seed: int = 0) -> dict:
    seeds = jax.random.split(jax.random.key(seed), 4)
    mobility = jnp.clip(jnp.exp(math.log(5.0) - 3.218876 * jax.random.uniform(seeds[0], (NX, NY, NZ), jnp.float32) ** level_of(seeds[0], (NX, NY, NZ), ((0, 128), (1, 4)), -0.2, 0.2)), 0.2, 5.0)
    sav_vector = draw_sav_vector(jax.random.fold_in(seeds[3], 71), 0)
    cotangent = draw_cotangent(jax.random.fold_in(seeds[3], 71), 0)
    return {"mobility": mobility, "sav_vector": sav_vector, "cotangent": cotangent}


DAMPING = 0.8
BASE_TAU = 16.0


def face_terms(padded, tau):
    center = padded[1:-1, 1:-1, 1:-1]
    others = [padded[2:, 1:-1, 1:-1], padded[:-2, 1:-1, 1:-1], padded[1:-1, 2:, 1:-1],
              padded[1:-1, :-2, 1:-1], padded[1:-1, 1:-1, 2:], padded[1:-1, 1:-1, :-2]]
    couplings = jnp.stack([(0.5 * tau) * (center + other) for other in others]).astype(jnp.bfloat16)
    diagonal = jnp.float32(1.0) + couplings[0].astype(jnp.float32)
    for index in range(1, 6):
        diagonal = diagonal + couplings[index].astype(jnp.float32)
    return couplings, diagonal


def coarsen(values):
    count, size_x, size_y, size_z = values.shape
    blocks = values.reshape(count, size_x // 2, 2, size_y // 2, 2, size_z // 2, 2)
    return blocks.mean(axis=(2, 4, 6))


def refine(values):
    return jnp.repeat(jnp.repeat(jnp.repeat(values, 2, axis=1), 2, axis=2), 2, axis=3)


def operate(iterate, couplings, diagonal):
    padded = jnp.pad(iterate, ((0, 0), (1, 1), (1, 1), (1, 1)))
    others = [padded[:, 2:, 1:-1, 1:-1], padded[:, :-2, 1:-1, 1:-1], padded[:, 1:-1, 2:, 1:-1],
              padded[:, 1:-1, :-2, 1:-1], padded[:, 1:-1, 1:-1, 2:], padded[:, 1:-1, 1:-1, :-2]]
    total = couplings[0].astype(jnp.float32)[None] * others[0]
    for index in range(1, 6):
        total = total + couplings[index].astype(jnp.float32)[None] * others[index]
    return diagonal[None] * iterate - total


def relax_once(iterate, source, couplings, diagonal):
    return iterate + DAMPING * (source - operate(iterate, couplings, diagonal)) / diagonal[None]


def multigrid(source, level_index, operators):
    couplings, diagonal = operators[level_index]
    iterate = DAMPING * source / diagonal[None]
    if level_index == LEVELS - 1:
        return relax_once(iterate, source, couplings, diagonal)
    iterate = relax_once(iterate, source, couplings, diagonal)
    residual = source - operate(iterate, couplings, diagonal)
    correction = multigrid(coarsen(residual), level_index + 1, operators)
    iterate = iterate + refine(correction)
    iterate = relax_once(iterate, source, couplings, diagonal)
    return relax_once(iterate, source, couplings, diagonal)


def reference(mobility, sav_vector, cotangent):
    operators = []
    mobile = mobility
    for level_index in range(LEVELS):
        operators.append(face_terms(jnp.pad(mobile, 1), BASE_TAU / 4.0 ** level_index))
        if level_index + 1 < LEVELS:
            mobile = coarsen(mobile[None])[0]
    adjoint_b = multigrid(sav_vector[None], 0, operators)[0]
    numerator = jnp.sum(adjoint_b * cotangent)
    denominator = jnp.sum(sav_vector * adjoint_b)
    sav_ratio = numerator / (1.0 + denominator)
    return multigrid((cotangent - sav_ratio * sav_vector)[None], 0, operators)[0]
```

```python
import functools

import jax
import jax.numpy as jnp
from jax import lax
from jax.experimental import pallas as pl
from jax.experimental.pallas import tpu as pltpu
from jax.sharding import PartitionSpec as P

f32 = jnp.float32
HALO = 4
DAMPING = 0.8
BASE_TAU = 16.0
VMEM = pl.BlockSpec(memory_space=pltpu.VMEM)


def half_tau(level):
    return 0.5 * BASE_TAU / 4.0**level


def iota(shape, dim):
    return lax.broadcasted_iota(jnp.int32, shape, dim)


def dot(a, b):
    return jnp.dot(a, b, precision=lax.Precision.HIGHEST, preferred_element_type=f32)


def rounded(x):
    return x.astype(jnp.bfloat16).astype(f32)


def ahead(x, axis):
    return pltpu.roll(x, x.shape[axis] - 1, axis)


def behind(x, axis):
    return pltpu.roll(x, 1, axis)


def coefficients(level, m, cx, cy, cz, dg, wt, rows, y_len, z_len, z_fields):
    shape = m.shape[1:]
    tau = half_tau(level)
    lane = iota(shape, 1)
    z_last = lax.rem(lane, z_len) == z_len - 1
    z_first = lax.rem(lane, z_len) == 0
    sub = iota(shape, 0)

    def couple_x(i):
        return rounded(tau * (m[i] + m[i + 1]))

    cx[0] = couple_x(0)

    def body(i, _):
        here = m[i]
        edge = rounded(tau * here)
        x_up = couple_x(i)
        cx[i] = x_up
        y_up = rounded(tau * (here + ahead(here, 0)))
        if y_len is None:
            y_down = behind(y_up, 0)
            cy[i] = y_up
        else:
            inner = jnp.where(sub >= y_len - 1, 0.0, y_up)
            y_up = jnp.where(sub == y_len - 1, edge, y_up)
            y_down = jnp.where(sub == 0, edge, behind(inner, 0))
            cy[i] = inner
        inner = jnp.where(z_last, 0.0, rounded(tau * (here + ahead(here, 1))))
        cz[i] = inner
        z_up = jnp.where(z_last, edge, inner)
        z_down = jnp.where(z_first, edge, behind(inner, 1))
        diagonal = 1.0 + x_up + cx[i - 1] + y_up + y_down + z_up + z_down
        dg[i] = diagonal
        wt[i] = jnp.where(here > 0.0, DAMPING / diagonal, 0.0)
        return 0

    lax.fori_loop(1, rows - 1, body, 0)


def residual_row(i, r, v, cx, cy, cz, dg):
    here = v[i]
    up = cy[i]
    side = cz[i]
    total = cx[i] * v[i + 1] + cx[i - 1] * v[i - 1]
    total = total + (up * ahead(here, 0) + behind(up * here, 0))
    total = total + (side * ahead(here, 1) + behind(side * here, 1))
    return r - dg[i] * here + total


def sweep(lo, hi, source, v, out, coefs, wt, offset=0):
    def body(i, _):
        for s, a, o in zip(source, v, out):
            o[i] = a[i] + wt[i] * residual_row(i, s[i - offset], a, *coefs)
        return 0

    lax.fori_loop(lo, hi, body, 0)


def coarse_z(z_in, lanes_in, z_out, lanes_out, fields, shift=0, single=False):
    src = iota((lanes_in, lanes_out), 0)
    dst = iota((lanes_in, lanes_out), 1)
    target = lax.div(src, z_in) * z_out + lax.div(lax.rem(src, z_in), 2) + shift
    return jnp.where((target == dst) & (src < fields * z_in), 0.125, 0.0).astype(f32)


def fine_z(z_in, lanes_in, z_out, lanes_out, fields, shift=0):
    src = iota((lanes_in, lanes_out), 0)
    dst = iota((lanes_in, lanes_out), 1)
    wanted = lax.div(dst, z_out) * z_in + lax.div(lax.rem(dst, z_out), 2) + shift
    return jnp.where((wanted == src) & (dst < fields * z_out), 1.0, 0.0).astype(f32)


def down0(own, xlo, xhi, out, vs, vc, cx, cy, cz, dg, wt, ss, cc, m, us, uc, pair, thin):
    for index, ref in enumerate((m, ss, cc)):

        def copy_edge(i, _, index=index, ref=ref):
            ref[i] = xlo[index, i]
            ref[i + 20] = xhi[index, i]
            return 0

        def copy_own(i, _, index=index, ref=ref):
            ref[i + 4] = own[index, i]
            return 0

        lax.fori_loop(0, 4, copy_edge, 0)
        lax.fori_loop(0, 16, copy_own, 0)
    coefficients(0, m, cx, cy, cz, dg, wt, 24, None, 256, 1)
    coefs = (cx, cy, cz, dg)

    def first(i, _):
        us[i] = wt[i] * ss[i]
        uc[i] = wt[i] * cc[i]
        return 0

    lax.fori_loop(1, 23, first, 0)
    sweep(2, 22, (ss, cc), (us, uc), (vs, vc), coefs, wt)
    for ref in (vs, vc):
        for row in (0, 1, 22, 23):
            ref[row] = jnp.zeros((24, 256), f32)

    def rest(k, sums):
        num, den = sums
        folded = [0.0, 0.0]
        for half in range(2):
            i = 4 + 2 * k + half
            res_s = residual_row(i, ss[i], vs, *coefs)
            res_c = residual_row(i, cc[i], vc, *coefs)
            num = num + (vs[i] * cc[i] + res_s * vc[i])
            den = den + (vs[i] * ss[i] + res_s * vs[i])
            folded[0] = folded[0] + res_s
            folded[1] = folded[1] + res_c
        pair[k] = folded[0]
        pair[k + 8] = folded[1]
        pair[k + 16] = m[4 + 2 * k] + m[5 + 2 * k]
        return num, den

    zero = jnp.zeros((24, 256), f32)
    num, den = lax.fori_loop(0, 8, rest, (zero, zero))
    thin[...] = dot(pair[...].reshape(576, 256), coarse_z(256, 256, 128, 128, 1))

    def fold(k, _):
        value = thin[pl.ds(k * 24 + 4, 8, stride=2), :] + thin[pl.ds(k * 24 + 5, 8, stride=2), :]
        for j in range(4):
            out[j, k] = value
        return 0

    lax.fori_loop(0, 24, fold, 0)
    sub = iota((24, 256), 0)
    inside = (sub >= 4) & (sub < 20)
    num = jnp.sum(jnp.where(inside, num, 0.0))
    den = jnp.sum(jnp.where(inside, den, 0.0))
    lane = iota((8, 128), 1)
    both = jnp.where(lane == 0, num, jnp.where(lane == 1, den, 0.0))
    for j in range(4):
        out[j, 24] = both


def down1(lo, own, hi, to_up, to_down, mine, sums, vs, vc, cx, cy, cz, dg, wt, ss, cc, m, us, uc, pair, thin):
    for part, ref in enumerate((lo, own, hi)):

        def copy(i, _, part=part, ref=ref):
            for j in range(4):
                for index, target in enumerate((ss, cc, m)):
                    target[2 + part * 8 + i, pl.ds(8 * j, 8), :] = ref[j, index * 8 + i]
            return 0

        lax.fori_loop(0, 8, copy, 0)
    for ref in (ss, cc, m, vs, vc):
        for row in (0, 1, 26, 27):
            ref[row] = jnp.zeros((32, 128), f32)
    coefficients(1, m, cx, cy, cz, dg, wt, 28, 32, 128, 1)
    coefs = (cx, cy, cz, dg)

    def first(i, _):
        us[i] = wt[i] * ss[i]
        uc[i] = wt[i] * cc[i]
        return 0

    lax.fori_loop(1, 27, first, 0)
    sweep(2, 26, (ss, cc), (us, uc), (vs, vc), coefs, wt)

    def rest(k, sums):
        num, den = sums
        folded = [0.0, 0.0]
        mask = jnp.where((k >= 4) & (k < 8), 1.0, 0.0)
        for half in range(2):
            i = 2 + 2 * k + half
            res_s = residual_row(i, ss[i], vs, *coefs)
            res_c = residual_row(i, cc[i], vc, *coefs)
            num = num + mask * (vs[i] * cc[i] + res_s * vc[i])
            den = den + mask * (vs[i] * ss[i] + res_s * vs[i])
            folded[0] = folded[0] + res_s
            folded[1] = folded[1] + res_c
        pair[k, :, 0:128] = folded[0]
        pair[k, :, 128:256] = folded[1]
        return num, den

    zero = jnp.zeros((32, 128), f32)
    num, den = lax.fori_loop(0, 12, rest, (zero, zero))

    def rest_m(k, _):
        both = m[2 * k + 2] + m[2 * k + 3]
        pair[k + 12, :, 0:128] = both
        pair[k + 12, :, 128:256] = both
        return 0

    lax.fori_loop(0, 12, rest_m, 0)
    thin[...] = dot(pair[...].reshape(768, 256), coarse_z(128, 256, 64, 128, 2))

    def folded_row(k):
        return thin[pl.ds(k * 32, 16, stride=2), :] + thin[pl.ds(k * 32 + 1, 16, stride=2), :]

    place = lax.axis_index("wide")
    for k in range(12):
        value = folded_row(k)
        if k < 2:
            value = jnp.where(place == 1, value, 0.0)
        elif k >= 10:
            value = jnp.where(place == lax.axis_size("wide") - 2, value, 0.0)
        mine[k] = value
        if k < 10:
            to_up[k] = value
        if k >= 2:
            to_down[k - 2] = value

    def fold_m(k, _):
        mine[k + 12] = folded_row(k + 12)
        return 0

    lax.fori_loop(0, 12, fold_m, 0)
    lane = iota((16, 128), 1)
    for k in range(4):
        to_up[10 + k] = jnp.where(lane < 64, mine[12 + k], mine[16 + k])
        to_down[10 + k] = jnp.where(lane < 64, mine[16 + k], mine[20 + k])
    lane = iota((8, 128), 1)
    num = jnp.sum(num) * 8.0
    den = jnp.sum(den) * 8.0
    finer = own[0, 24] + own[1, 24] + own[2, 24] + own[3, 24]
    sums[...] = finer + jnp.where(lane == 0, num, jnp.where(lane == 1, den, 0.0))


def bottom(
    dn4, dn2, mine, up2, up4, finer, e2, sums,
    m2, r2, u2, v2, cx2, cy2, cz2, dg2, wt2,
    m3, r3, u3, v3, cx3, cy3, cz3, dg3, wt3,
    m4, r4, u4, v4, cx4, cy4, cz4, dg4, wt4,
    pair, thin, wide, add,
):
    lane16 = iota((16, 128), 1)

    def unpack(ref, first, r_at, m_at):
        def body(k, _):
            r2[r_at + k] = ref[first + k]
            return 0

        lax.fori_loop(0, 8, body, 0)

        def body_m(k, _):
            packed = ref[10 + k]
            other = pltpu.roll(packed, 64, 1)
            m2[m_at + k] = jnp.where(lane16 < 64, packed, other)
            m2[m_at + 4 + k] = jnp.where(lane16 < 64, other, packed)
            return 0

        lax.fori_loop(0, 4, body_m, 0)

    unpack(dn4, 2, 2, 0)
    unpack(dn2, 2, 10, 8)
    unpack(up2, 0, 26, 28)
    unpack(up4, 0, 34, 36)
    for k in range(2):
        r2[8 + k] = r2[8 + k] + dn2[k]
        r2[16 + k] = r2[16 + k] + mine[k]
        r2[26 + k] = r2[26 + k] + mine[10 + k]
        r2[34 + k] = r2[34 + k] + up2[8 + k]

    def body_own(k, _):
        r2[18 + k] = mine[2 + k]
        return 0

    lax.fori_loop(0, 8, body_own, 0)

    def body_own_m(k, _):
        m2[16 + k] = mine[12 + k]
        return 0

    lax.fori_loop(0, 12, body_own_m, 0)

    def relax(level, m, r, u, v, cx, cy, cz, dg, wt, rows, y_len, z_len, r_lo, r_hi):
        coefficients(level, m, cx, cy, cz, dg, wt, rows, y_len, z_len, 2)

        def first(i, _):
            u[i] = wt[i] * r[i]
            return 0

        lax.fori_loop(r_lo, r_hi, first, 0)
        sweep(r_lo + 1, r_hi - 1, (r,), (u,), (v,), (cx, cy, cz, dg), wt)

    def products(i, r, v, res, z_len):
        num = v * pltpu.roll(r, 128 - z_len, 1)
        den = v * r
        if res is not None:
            num = num + res * pltpu.roll(v, 128 - z_len, 1)
            den = den + res * v
        lane = iota(v.shape, 1)
        return jnp.where(lane < z_len, num, 0.0), jnp.where(lane < z_len, den, 0.0)

    def restrict(m, r, v, coefs, k_count, m_count, y_in, m_next, r_next, r_at, z_len, own_lo, own_hi):
        shape = r.shape[1:]

        def rest(k, sums):
            num, den = sums
            total = 0.0
            mask = jnp.where((k >= own_lo) & (k < own_hi), 1.0, 0.0)
            for half in range(2):
                i = 4 + 2 * k + half
                res = residual_row(i, r[i], v, *coefs)
                a, b = products(i, r[i], v[i], res, z_len)
                num = num + mask * a
                den = den + mask * b
                total = total + res
            pair[pl.ds(pl.multiple_of(k * y_in, 8), y_in), :] = total
            return num, den

        zero = jnp.zeros(shape, f32)
        num, den = lax.fori_loop(0, k_count, rest, (zero, zero))

        def rest_m(k, _):
            pair[pl.ds(pl.multiple_of((k_count + k) * y_in, 8), y_in), :] = m[2 * k] + m[2 * k + 1]
            return 0

        lax.fori_loop(0, m_count, rest_m, 0)
        n = (k_count + m_count) * y_in
        thin[0:n, :] = dot(pair[0:n, :], coarse_z(z_len, 128, z_len // 2, 128, 2))
        y_out = y_in // 2

        def folded(k):
            return (
                thin[pl.ds(k * y_in, y_out, stride=2), :] + thin[pl.ds(k * y_in + 1, y_out, stride=2), :]
            )

        def fold(k, _):
            r_next[r_at + k, 0:y_out, :] = folded(k)
            return 0

        def fold_m(k, _):
            m_next[k, 0:y_out, :] = folded(k_count + k)
            return 0

        lax.fori_loop(0, k_count, fold, 0)
        lax.fori_loop(0, m_count, fold_m, 0)
        return jnp.sum(num), jnp.sum(den)

    c2 = (cx2, cy2, cz2, dg2)
    c3 = (cx3, cy3, cz3, dg3)
    c4 = (cx4, cy4, cz4, dg4)
    relax(2, m2, r2, u2, v2, *c2, wt2, 44, 16, 64, 2, 42)
    num2, den2 = restrict(m2, r2, v2, c2, 18, 22, 16, m3, r3, 2, 64, 8, 10)
    relax(3, m3, r3, u3, v3, *c3, wt3, 22, 8, 32, 2, 20)
    m4[...] = jnp.zeros((11, 8, 128), f32)
    r4[...] = jnp.zeros((11, 8, 128), f32)
    num3, den3 = restrict(m3, r3, v3, c3, 7, 11, 8, m4, r4, 2, 32, 3, 4)
    relax(4, m4, r4, u4, v4, *c4, wt4, 11, 4, 16, 2, 9)
    a4, b4 = products(5, r4[5], v4[5], None, 16)
    num = 64.0 * num2 + 512.0 * num3 + 4096.0 * jnp.sum(a4)
    den = 64.0 * den2 + 512.0 * den3 + 4096.0 * jnp.sum(b4)
    lane = iota((8, 128), 1)
    total = finer[...] + jnp.where(lane == 0, num, jnp.where(lane == 1, den, 0.0))
    sums[...] = jnp.broadcast_to(total[0:1].reshape(1, 1, 128), sums.shape)

    def correct(k_lo, k_hi, coarse, y_in, v, at, z_len):
        y_out = 2 * y_in

        def body(k, _):
            value = coarse[k, 0:y_in, :]
            base = pl.multiple_of((k - k_lo) * y_out, 8)
            wide[pl.ds(base, y_in, stride=2), :] = value
            wide[pl.ds(base + 1, y_in, stride=2), :] = value
            return 0

        lax.fori_loop(k_lo, k_hi, body, 0)
        n = (k_hi - k_lo) * y_out
        add[0:n, :] = dot(wide[0:n, :], fine_z(z_len // 2, 128, z_len, 128, 2))

        def body_add(k, _):
            value = add[pl.ds(pl.multiple_of(k * y_out, 8), y_out), :]
            v[at + 2 * k] = v[at + 2 * k] + value
            v[at + 2 * k + 1] = v[at + 2 * k + 1] + value
            return 0

        lax.fori_loop(0, k_hi - k_lo, body_add, 0)

    correct(3, 8, v4, 4, v3, 6, 32)
    sweep(7, 15, (r3,), (v3,), (u3,), c3, wt3)
    sweep(8, 14, (r3,), (u3,), (v3,), c3, wt3)
    correct(8, 14, v3, 8, v2, 16, 64)
    sweep(17, 27, (r2,), (v2,), (u2,), c2, wt2)

    def last(i, _):
        e2[i - 18] = u2[i] + wt2[i] * residual_row(i, r2[i], u2, *c2)
        return 0

    lax.fori_loop(18, 26, last, 0)


def up(
    e2, vs1, vc1, cx1, cy1, cz1, dg1, wt1, ss1, cc1, vs0, vc0, cx0, cy0, cz0, dg0, wt0, ss0, cc0,
    out_s, out_c, as1, ac1, bs1, bc1, as0, ac0, bs0, bc0, wide, add, block, thick, full,
):
    c1 = (cx1, cy1, cz1, dg1)
    c0 = (cx0, cy0, cz0, dg0)

    def widen(k, _):
        value = e2[k]
        wide[pl.ds(k * 32, 16, stride=2), :] = value
        wide[pl.ds(k * 32 + 1, 16, stride=2), :] = value
        return 0

    lax.fori_loop(0, 8, widen, 0)
    add[...] = dot(wide[...], fine_z(64, 128, 128, 256, 2))

    def correct1(k, _):
        both = add[pl.ds(pl.multiple_of(k * 32, 8), 32), :]
        for half in range(2):
            i = 6 + 2 * k + half
            as1[i] = vs1[i] + both[:, 0:128]
            ac1[i] = vc1[i] + both[:, 128:256]
        return 0

    lax.fori_loop(0, 8, correct1, 0)
    sweep(8, 20, (ss1, cc1), (as1, ac1), (bs1, bc1), c1, wt1)
    place = lax.axis_index("narrow")
    block[...] = jnp.zeros((960, 128), f32)

    def last1(i, _):
        for index, (r, v) in enumerate(((ss1, bs1), (cc1, bc1))):
            value = v[i] + wt1[i] * residual_row(i, r[i], v, *c1)
            block[pl.ds(pl.multiple_of((index * 10 + i - 9) * 48 + 8, 8), 32), :] = value
        return 0

    lax.fori_loop(9, 19, last1, 0)

    def take(k, _):
        value = block[pl.ds(pl.multiple_of(k * 48 + 8 * place, 8), 24), :][6:18, :]
        thick[pl.ds(k * 24, 12, stride=2), :] = value
        thick[pl.ds(k * 24 + 1, 12, stride=2), :] = value
        return 0

    lax.fori_loop(0, 20, take, 0)
    full[...] = dot(thick[...], fine_z(128, 128, 256, 256, 1)).reshape(20, 24, 256)

    def correct0(k, _):
        for half in range(2):
            i = 2 + 2 * k + half
            as0[i] = vs0[i] + full[k]
            ac0[i] = vc0[i] + full[10 + k]
        return 0

    lax.fori_loop(0, 10, correct0, 0)
    sweep(3, 21, (ss0, cc0), (as0, ac0), (bs0, bc0), c0, wt0)

    def last0(i, _):
        for r, v, o in ((ss0, bs0, out_s), (cc0, bc0, out_c)):
            value = v[i] + wt0[i] * residual_row(i, r[i], v, *c0)
            o[i - 4] = value[4:20, :]
        return 0

    lax.fori_loop(4, 20, last0, 0)


def call(kernel, ins, outs, scratch, name):
    return pl.pallas_call(
        kernel,
        out_shape=[jax.ShapeDtypeStruct(s, f32) for s in outs],
        in_specs=[VMEM] * len(ins),
        out_specs=[VMEM] * len(outs),
        scratch_shapes=[pltpu.VMEM(s, f32) for s in scratch],
        compiler_params=pltpu.CompilerParams(vmem_limit_bytes=40 * 2**20),
        name=name,
    )(*ins)


def shifted(value, axis, by):
    size = lax.axis_size(axis)
    return lax.ppermute(value, axis, [(i, i + by) for i in range(size) if 0 <= i + by < size])


def per_device(mobility, sav_vector, cotangent):
    own = jnp.stack([mobility, sav_vector, cotangent])
    y_lo = shifted(own[:, :, -HALO:], "narrow", 1)
    y_hi = shifted(own[:, :, :HALO], "narrow", -1)
    own = jnp.concatenate([y_lo, own, y_hi], axis=2)
    x_lo = shifted(own[:, -HALO:], "wide", 1)
    x_hi = shifted(own[:, :HALO], "wide", -1)
    a0 = (24, 24, 256)
    chunk, *state0 = call(
        down0,
        (own, x_lo, x_hi),
        [(4, 25, 8, 128)] + [a0] * 9,
        [a0] * 4 + [(576, 128)],
        "down0",
    )
    gathered = lax.all_to_all(chunk, "narrow", 0, 0)
    lo = shifted(gathered, "wide", 1)
    hi = shifted(gathered, "wide", -1)
    a1 = (28, 32, 128)
    to_up, to_down, mine, finer, *state1 = call(
        down1,
        (lo, gathered, hi),
        [(14, 16, 128), (14, 16, 128), (24, 16, 128), (8, 128)] + [a1] * 9,
        [a1] * 3 + [(24, 32, 256), (768, 128)],
        "down1",
    )
    dn2 = shifted(to_up, "wide", 2)
    up2 = shifted(to_down, "wide", -2)
    dn4 = shifted(to_up, "wide", 4)
    up4 = shifted(to_down, "wide", -4)
    wide = lax.axis_size("wide")
    e2, sums = call(
        bottom,
        (dn4, dn2, mine, up2, up4, finer),
        [(8, 16, 128), (wide, 1, 128)],
        [(44, 16, 128)] * 9
        + [(22, 8, 128)] * 9
        + [(11, 8, 128)] * 9
        + [(640, 128), (640, 128), (96, 128), (96, 128)],
        "bottom",
    )
    every = lax.all_to_all(sums, "wide", 0, 0)
    out_s, out_c = call(
        up,
        (e2, *state1, *state0),
        [(16, 16, 256)] * 2,
        [a1] * 4 + [a0] * 4 + [(256, 128), (256, 256), (960, 128), (480, 128), (20, 24, 256)],
        "up",
    )
    totals = jnp.sum(every, axis=(0, 1))
    ratio = totals[0] / (1.0 + totals[1])
    return out_c - ratio * out_s


def solution(mesh):
    spec = P("wide", "narrow", None)
    return jax.shard_map(
        per_device, mesh=mesh, in_specs=(spec, spec, spec), out_specs=spec, check_vma=False
    )
```

```python
import functools

import jax
import jax.numpy as jnp
from jax import lax
from jax.experimental import pallas as pl
from jax.experimental.pallas import tpu as pltpu
from jax.sharding import PartitionSpec as P

f32 = jnp.float32
HALO = 4
LIMIT = 24
DAMPING = 0.8
BASE_TAU = 16.0
VMEM = pl.BlockSpec(memory_space=pltpu.VMEM)
HBM = pl.BlockSpec(memory_space=pltpu.HBM)


def half_tau(level):
    return 0.5 * BASE_TAU / 4.0**level


def iota(shape, dim):
    return lax.broadcasted_iota(jnp.int32, shape, dim)


def dot(a, b):
    return jnp.dot(a, b, precision=lax.Precision.HIGHEST, preferred_element_type=f32)


def rounded(x):
    return x.astype(jnp.bfloat16).astype(f32)


def ahead(x, axis):
    return pltpu.roll(x, x.shape[axis] - 1, axis)


def behind(x, axis):
    return pltpu.roll(x, 1, axis)


def at(i, n):
    return pl.ds(i, n) if n > 1 or not isinstance(i, int) else slice(i, i + 1)


def by_rows(lo, hi, n, fn, carry=None):
    count = (hi - lo) // n
    if count > 1:
        carry = lax.fori_loop(0, count, lambda t, c: fn(lo + t * n, n, c), carry)
    elif count == 1:
        carry = fn(lo, n, carry)
    rest = hi - lo - count * n
    if rest:
        carry = fn(lo + count * n, rest, carry)
    return carry


def coefficients(level, m, cx, cy, cz, dg, wt, lo, hi, n, y_len, z_len):
    tau = half_tau(level)
    cx[lo - 1] = rounded(tau * (m[lo - 1] + m[lo]))

    def body(i, n, carry):
        here = m[at(i, n)]
        shape = here.shape
        lane = lax.rem(iota(shape, 2), z_len)
        z_last = lane == z_len - 1
        z_first = lane == 0
        edge = rounded(tau * here)
        x_up = rounded(tau * (here + m[at(i + 1, n)]))
        cx[at(i, n)] = x_up
        y_up = rounded(tau * (here + ahead(here, 1)))
        if y_len is None:
            y_down = behind(y_up, 1)
            cy[at(i, n)] = y_up
        else:
            sub = iota(shape, 1)
            inner = jnp.where(sub >= y_len - 1, 0.0, y_up)
            y_up = jnp.where(sub == y_len - 1, edge, y_up)
            y_down = jnp.where(sub == 0, edge, behind(inner, 1))
            cy[at(i, n)] = inner
        inner = jnp.where(z_last, 0.0, rounded(tau * (here + ahead(here, 2))))
        cz[at(i, n)] = inner
        z_up = jnp.where(z_last, edge, inner)
        z_down = jnp.where(z_first, edge, behind(inner, 2))
        diagonal = 1.0 + x_up + cx[at(i - 1, n)] + y_up + y_down + z_up + z_down
        if dg is not None:
            dg[at(i, n)] = diagonal
        wt[at(i, n)] = jnp.where(here > 0.0, DAMPING / diagonal, 0.0)
        return carry

    by_rows(lo, hi, n, body, 0)


def coupled(i, n, v, cx, cy, cz):
    here = v[at(i, n)]
    up = cy[at(i, n)]
    side = cz[at(i, n)]
    total = cx[at(i, n)] * v[at(i + 1, n)] + cx[at(i - 1, n)] * v[at(i - 1, n)]
    total = total + (up * ahead(here, 1) + behind(up * here, 1))
    return total + (side * ahead(here, 2) + behind(side * here, 2))


def residual(i, n, r, v, cx, cy, cz, dg):
    return r - dg[at(i, n)] * v[at(i, n)] + coupled(i, n, v, cx, cy, cz)


def relaxed(i, n, r, v, wt, cx, cy, cz, *_):
    return (1.0 - DAMPING) * v[at(i, n)] + wt[at(i, n)] * (r[at(i, n)] + coupled(i, n, v, cx, cy, cz))


def start(lo, hi, n, source, out, wt):
    def body(i, n, carry):
        for s, o in zip(source, out):
            o[at(i, n)] = wt[at(i, n)] * s[at(i, n)]
        return carry

    by_rows(lo, hi, n, body, 0)


def sweep(lo, hi, n, source, v, out, coefs, wt):
    def body(i, n, carry):
        for s, a, o in zip(source, v, out):
            o[at(i, n)] = relaxed(i, n, s, a, wt, *coefs)
        return carry

    by_rows(lo, hi, n, body, 0)


def pairs(x):
    x = x.reshape(x.shape[0] // 2, 2, *x.shape[1:])
    return x[:, 0] + x[:, 1]


def doubled(x):
    x = jnp.broadcast_to(x[:, None], (x.shape[0], 2, *x.shape[1:]))
    return x.reshape(x.shape[0] * 2, *x.shape[2:])


def flat_dot(x, matrix):
    n = x.shape[0] * x.shape[1]
    return dot(x.reshape(n, x.shape[2]), matrix).reshape(x.shape[0], x.shape[1], matrix.shape[1])


def fold_y(ref, k, n, first, count):
    return ref[k : k + n, pl.ds(first, count, stride=2), :] + ref[k : k + n, pl.ds(first + 1, count, stride=2), :]


def coarse_z(z_in, lanes_in, z_out, lanes_out, fields):
    src = iota((lanes_in, lanes_out), 0)
    dst = iota((lanes_in, lanes_out), 1)
    target = lax.div(src, z_in) * z_out + lax.div(lax.rem(src, z_in), 2)
    return jnp.where((target == dst) & (src < fields * z_in), 0.125, 0.0).astype(f32)


def fine_z(z_in, lanes_in, z_out, lanes_out, fields):
    src = iota((lanes_in, lanes_out), 0)
    dst = iota((lanes_in, lanes_out), 1)
    wanted = lax.div(dst, z_out) * z_in + lax.div(lax.rem(dst, z_out), 2)
    return jnp.where((wanted == src) & (dst < fields * z_out), 1.0, 0.0).astype(f32)


def products(i, n, s, c, us, uc, coefs, sums):
    num, den = sums
    v_s, v_c = us[at(i, n)], uc[at(i, n)]
    r_s, r_c = s[at(i, n)], c[at(i, n)]
    res_s = residual(i, n, r_s, us, *coefs)
    res_c = residual(i, n, r_c, uc, *coefs)
    num = num + jnp.sum(v_s * r_c + res_s * v_c, axis=0)
    den = den + jnp.sum(v_s * r_s + res_s * v_s, axis=0)
    return res_s, res_c, (num, den)


def fetch(sources, targets, sems):
    copies = [pltpu.make_async_copy(a, b, sems.at[k]) for k, (a, b) in enumerate(zip(sources, targets))]
    for copy in copies:
        copy.start()
    return copies


def wait(copies):
    for copy in copies:
        copy.wait()


def fetch0(own, xlo, xhi, fields, sems):
    sources, targets = [], []
    for index, ref in enumerate(fields):
        for part, lo, hi in ((xlo, 0, 4), (own, 4, 20), (xhi, 20, 24)):
            sources.append(part.at[index])
            targets.append(ref.at[pl.ds(lo, hi - lo)])
    return fetch(sources, targets, sems)


def fetch1(lo, own, hi, fields, sems):
    sources, targets = [], []
    for index, ref in fields:
        for part, source in enumerate((lo, own, hi)):
            for j in range(4):
                sources.append(source.at[j, pl.ds(index * 8, 8)])
                targets.append(ref.at[pl.ds(2 + part * 8, 8), pl.ds(8 * j, 8), :])
    return fetch(sources, targets, sems)


def down0(own, xlo, xhi, out, vs, vc, cx, cy, cz, dg, wt, ss, cc, m, us, uc, pair, thin, sems):
    copies = fetch0(own, xlo, xhi, (m, ss, cc), sems)
    wait(copies[:3])
    coefficients(0, m, cx, cy, cz, dg, wt, 1, 23, 2, None, 256)
    coefs = (cx, cy, cz, dg)
    wait(copies[3:])
    start(1, 23, 2, (ss, cc), (us, uc), wt)
    sweep(2, 22, 2, (ss, cc), (us, uc), (vs, vc), coefs, wt)

    def rest(i, n, sums):
        res_s, res_c, sums = products(i, n, ss, cc, vs, vc, coefs, sums)
        k = lax.div(i - 4, 2)
        pair[at(k, n // 2)] = pairs(res_s)
        pair[at(k + 8, n // 2)] = pairs(res_c)
        pair[at(k + 16, n // 2)] = pairs(m[at(i, n)])
        return sums

    zero = jnp.zeros((24, 256), f32)
    num, den = by_rows(4, 20, 2, rest, (zero, zero))
    thin[...] = flat_dot(pair[...], coarse_z(256, 256, 128, 128, 1))
    value = fold_y(thin, 0, 24, 4, 8)
    sub = iota((24, 256), 0)
    inside = (sub >= 4) & (sub < 20)
    num = jnp.sum(jnp.where(inside, num, 0.0))
    den = jnp.sum(jnp.where(inside, den, 0.0))
    lane = iota((8, 128), 1)
    both = jnp.where(lane == 0, num, jnp.where(lane == 1, den, 0.0))
    for j in range(4):
        out[j, 0:24] = value
        out[j, 24] = both


def down1(
    lo, own, hi, to_up, to_down, mine, sums,
    vs, vc, cx, cy, cz, dg, wt, ss, cc, m, us, uc, pair, thin, inner, sems,
):
    copies = fetch1(lo, own, hi, ((2, m), (0, ss), (1, cc)), sems)
    partial = fetch([own.at[j, 24] for j in range(4)], [inner.at[j] for j in range(4)], sems.at[pl.ds(36, 4)])
    for ref in (ss, cc, m, vs, vc):
        ref[0:2] = jnp.zeros((2, 32, 128), f32)
        ref[26:28] = jnp.zeros((2, 32, 128), f32)
    wait(copies[:12])
    coefficients(1, m, cx, cy, cz, dg, wt, 1, 27, 2, 32, 128)
    coefs = (cx, cy, cz, dg)
    wait(copies[12:])
    wait(partial)
    start(1, 27, 2, (ss, cc), (us, uc), wt)
    sweep(2, 26, 4, (ss, cc), (us, uc), (vs, vc), coefs, wt)

    def rest(i, n, sums):
        res_s, res_c, sums = products(i, n, ss, cc, vs, vc, coefs, sums)
        k = lax.div(i - 2, 2)
        pair[at(k, n // 2), :, 0:128] = pairs(res_s)
        pair[at(k, n // 2), :, 128:256] = pairs(res_c)
        both = pairs(m[at(i, n)])
        pair[at(k + 12, n // 2), :, 0:128] = both
        pair[at(k + 12, n // 2), :, 128:256] = both
        return sums

    zero = jnp.zeros((32, 128), f32)
    by_rows(2, 10, 4, rest, (zero, zero))
    num, den = by_rows(10, 18, 4, rest, (zero, zero))
    by_rows(18, 26, 4, rest, (zero, zero))
    thin[...] = flat_dot(pair[...], coarse_z(128, 256, 64, 128, 2))
    place = lax.axis_index("wide")
    low = jnp.where(place == 1, fold_y(thin, 0, 2, 0, 16), 0.0)
    mid = fold_y(thin, 2, 8, 0, 16)
    high = jnp.where(place == lax.axis_size("wide") - 2, fold_y(thin, 10, 2, 0, 16), 0.0)
    mob = fold_y(thin, 12, 12, 0, 16)
    mine[0:2] = low
    mine[2:10] = mid
    mine[10:12] = high
    mine[12:24] = mob
    to_up[0:2] = low
    to_up[2:10] = mid
    to_down[0:8] = mid
    to_down[8:10] = high
    left = iota((4, 16, 128), 2) < 64
    to_up[10:14] = jnp.where(left, mob[0:4], mob[4:8])
    to_down[10:14] = jnp.where(left, mob[4:8], mob[8:12])
    lane = iota((8, 128), 1)
    num = jnp.sum(num) * 8.0
    den = jnp.sum(den) * 8.0
    finer = inner[0] + inner[1] + inner[2] + inner[3]
    sums[...] = finer + jnp.where(lane == 0, num, jnp.where(lane == 1, den, 0.0))


def bottom(
    dn4, dn2, mine, up2, up4, finer, e2, sums,
    m2, r2, u2, v2, cx2, cy2, cz2, dg2, wt2,
    m3, r3, u3, v3, cx3, cy3, cz3, dg3, wt3,
    m4, r4, u4, v4, cx4, cy4, cz4, dg4, wt4,
    pair2, thin2, pair3, thin3, wide3, wide2,
):
    left = iota((4, 16, 128), 2) < 64

    def unpack(ref, first, r_at, m_at):
        r2[r_at : r_at + 8] = ref[first : first + 8]
        packed = ref[10:14]
        other = pltpu.roll(packed, 64, 2)
        m2[m_at : m_at + 4] = jnp.where(left, packed, other)
        m2[m_at + 4 : m_at + 8] = jnp.where(left, other, packed)

    unpack(dn4, 2, 2, 0)
    unpack(dn2, 2, 10, 8)
    unpack(up2, 0, 26, 28)
    unpack(up4, 0, 34, 36)
    r2[18:26] = mine[2:10]
    m2[16:28] = mine[12:24]
    r2[8:10] = r2[8:10] + dn2[0:2]
    r2[16:18] = r2[16:18] + mine[0:2]
    r2[26:28] = r2[26:28] + mine[10:12]
    r2[34:36] = r2[34:36] + up2[8:10]

    def both_products(r, v, res, z_len):
        num = v * pltpu.roll(r, 128 - z_len, 2)
        den = v * r
        if res is not None:
            num = num + res * pltpu.roll(v, 128 - z_len, 2)
            den = den + res * v
        mask = iota(v.shape, 2) < z_len
        return jnp.sum(jnp.where(mask, num, 0.0)), jnp.sum(jnp.where(mask, den, 0.0))

    c2 = (cx2, cy2, cz2, dg2)
    c3 = (cx3, cy3, cz3, dg3)
    c4 = (cx4, cy4, cz4, dg4)
    coefficients(2, m2, *c2, wt2, 1, 43, 6, 16, 64)
    start(2, 42, 8, (r2,), (u2,), wt2)
    sweep(3, 41, 8, (r2,), (u2,), (v2,), c2, wt2)

    def rest2(i, n, sums):
        res = residual(i, n, r2[at(i, n)], v2, *c2)
        pair2[at(lax.div(i - 4, 2), n // 2)] = pairs(res)
        return sums

    by_rows(4, 40, 6, rest2, 0)
    own = slice(20, 24)
    num2, den2 = both_products(r2[own], v2[own], residual(20, 4, r2[own], v2, *c2), 64)
    pair2[18:40] = pairs(m2[...])
    thin2[...] = flat_dot(pair2[...], coarse_z(64, 128, 32, 128, 2))
    r3[2:20] = fold_y(thin2, 0, 18, 0, 8)
    m3[...] = fold_y(thin2, 18, 22, 0, 8)

    coefficients(3, m3, *c3, wt3, 1, 21, 10, 8, 32)
    start(2, 20, 18, (r3,), (u3,), wt3)
    sweep(3, 19, 16, (r3,), (u3,), (v3,), c3, wt3)
    res = residual(4, 14, r3[4:18], v3, *c3)
    num3, den3 = both_products(r3[10:12], v3[10:12], res[6:8], 32)
    pair3[0:7] = pairs(res)
    pair3[7:18] = pairs(m3[...])
    thin3[...] = flat_dot(pair3[...], coarse_z(32, 128, 16, 128, 2))
    m4[...] = jnp.zeros((11, 8, 128), f32)
    r4[...] = jnp.zeros((11, 8, 128), f32)
    r4[2:9, 0:4, :] = fold_y(thin3, 0, 7, 0, 4)
    m4[:, 0:4, :] = fold_y(thin3, 7, 11, 0, 4)

    coefficients(4, m4, *c4, wt4, 1, 10, 9, 4, 16)
    start(2, 9, 7, (r4,), (u4,), wt4)
    sweep(3, 8, 5, (r4,), (u4,), (v4,), c4, wt4)
    num4, den4 = both_products(r4[5:6], v4[5:6], None, 16)
    num = 64.0 * num2 + 512.0 * num3 + 4096.0 * num4
    den = 64.0 * den2 + 512.0 * den3 + 4096.0 * den4
    lane = iota((8, 128), 1)
    total = finer[...] + jnp.where(lane == 0, num, jnp.where(lane == 1, den, 0.0))
    sums[...] = jnp.broadcast_to(total[0:1].reshape(1, 1, 128), sums.shape)

    wide3[:, pl.ds(0, 4, stride=2), :] = v4[3:8, 0:4, :]
    wide3[:, pl.ds(1, 4, stride=2), :] = v4[3:8, 0:4, :]
    v3[6:16] = v3[6:16] + doubled(flat_dot(wide3[...], fine_z(16, 128, 32, 128, 2)))
    sweep(7, 15, 8, (r3,), (v3,), (u3,), c3, wt3)
    sweep(8, 14, 6, (r3,), (u3,), (v3,), c3, wt3)
    wide2[:, pl.ds(0, 8, stride=2), :] = v3[8:14]
    wide2[:, pl.ds(1, 8, stride=2), :] = v3[8:14]
    v2[16:28] = v2[16:28] + doubled(flat_dot(wide2[...], fine_z(32, 128, 64, 128, 2)))
    sweep(17, 27, 10, (r2,), (v2,), (u2,), c2, wt2)
    e2[...] = relaxed(18, 8, r2, u2, wt2, *c2)


def up(
    e2, lo1, own1, hi1, own0, xlo0, xhi0, out_s, out_c,
    vs1, vc1, cx1, cy1, cz1, wt1, ss1, cc1, m1, as1, ac1, bs1, bc1,
    vs0, vc0, cx0, cy0, cz0, wt0, ss0, cc0, m0, as0, ac0, bs0, bc0,
    wide, add, block, thick, full, sems,
):
    copies1 = fetch1(lo1, own1, hi1, ((2, m1), (0, ss1), (1, cc1)), sems)
    copies0 = fetch0(own0, xlo0, xhi0, (m0, ss0, cc0), sems.at[pl.ds(36, 9)])
    c1 = (cx1, cy1, cz1)
    c0 = (cx0, cy0, cz0)
    wait(copies1)
    coefficients(1, m1, cx1, cy1, cz1, None, wt1, 5, 23, 2, 32, 128)
    start(5, 23, 2, (ss1, cc1), (as1, ac1), wt1)
    sweep(6, 22, 4, (ss1, cc1), (as1, ac1), (vs1, vc1), c1, wt1)
    wait(copies0)
    coefficients(0, m0, cx0, cy0, cz0, None, wt0, 1, 23, 2, None, 256)
    start(1, 23, 2, (ss0, cc0), (as0, ac0), wt0)
    sweep(2, 22, 2, (ss0, cc0), (as0, ac0), (vs0, vc0), c0, wt0)
    wide[:, pl.ds(0, 16, stride=2), :] = e2[...]
    wide[:, pl.ds(1, 16, stride=2), :] = e2[...]
    add[...] = flat_dot(wide[...], fine_z(64, 128, 128, 256, 2))

    def correct1(i, n, carry):
        k = lax.div(i - 6, 2)
        both = add[at(k, n // 2)]
        as1[at(i, n)] = vs1[at(i, n)] + doubled(both[:, :, 0:128])
        ac1[at(i, n)] = vc1[at(i, n)] + doubled(both[:, :, 128:256])
        return carry

    by_rows(6, 22, 4, correct1, 0)
    sweep(8, 20, 4, (ss1, cc1), (as1, ac1), (bs1, bc1), c1, wt1)
    place = lax.axis_index("narrow")
    block[:, 0:8, :] = jnp.zeros((20, 8, 128), f32)
    block[:, 40:48, :] = jnp.zeros((20, 8, 128), f32)

    def last1(i, n, carry):
        for index, (r, v) in enumerate(((ss1, bs1), (cc1, bc1))):
            value = relaxed(i, n, r, v, wt1, *c1)
            block[at(index * 10 + i - 9, n), 8:40, :] = value
        return carry

    by_rows(9, 19, 5, last1, 0)
    value = block[:, pl.ds(pl.multiple_of(8 * place, 8), 24), :][:, 6:18, :]
    thick[:, pl.ds(0, 12, stride=2), :] = value
    thick[:, pl.ds(1, 12, stride=2), :] = value
    full[...] = flat_dot(thick[...], fine_z(128, 128, 256, 256, 1))

    def correct0(i, n, carry):
        k = lax.div(i - 2, 2)
        as0[at(i, n)] = vs0[at(i, n)] + doubled(full[at(k, n // 2)])
        ac0[at(i, n)] = vc0[at(i, n)] + doubled(full[at(10 + k, n // 2)])
        return carry

    by_rows(2, 22, 2, correct0, 0)
    sweep(3, 21, 2, (ss0, cc0), (as0, ac0), (bs0, bc0), c0, wt0)

    def last0(i, n, carry):
        for r, v, o in ((ss0, bs0, out_s), (cc0, bc0, out_c)):
            o[at(i - 4, n)] = relaxed(i, n, r, v, wt0, *c0)[:, 4:20, :]
        return carry

    by_rows(4, 20, 2, last0, 0)


def final(every, out_s, out_c, out):
    total = jnp.sum(every[...], axis=0)
    lane = iota((1, 128), 1)
    num = jnp.sum(jnp.where(lane == 0, total, 0.0), axis=1, keepdims=True)
    den = jnp.sum(jnp.where(lane == 1, total, 0.0), axis=1, keepdims=True)
    ratio = (num / (1.0 + den))[0, 0]
    out[...] = out_c[...] - ratio * out_s[...]


def call(kernel, ins, outs, scratch, name, sems=0, specs=None):
    scratch = [pltpu.VMEM(s, f32) for s in scratch]
    if sems:
        scratch.append(pltpu.SemaphoreType.DMA((sems,)))
    return pl.pallas_call(
        kernel,
        out_shape=[jax.ShapeDtypeStruct(s, f32) for s in outs],
        in_specs=specs or [VMEM] * len(ins),
        out_specs=[VMEM] * len(outs),
        scratch_shapes=scratch,
        compiler_params=pltpu.CompilerParams(vmem_limit_bytes=LIMIT * 2**20),
        name=name,
    )(*ins)


def shifted(value, axis, by):
    size = lax.axis_size(axis)
    return lax.ppermute(value, axis, [(i, i + by) for i in range(size) if 0 <= i + by < size])


def per_device(mobility, sav_vector, cotangent):
    own = jnp.stack([mobility, sav_vector, cotangent])
    y_lo = shifted(own[:, :, -HALO:], "narrow", 1)
    y_hi = shifted(own[:, :, :HALO], "narrow", -1)
    own = jnp.concatenate([y_lo, own, y_hi], axis=2)
    x_lo = shifted(own[:, -HALO:], "wide", 1)
    x_hi = shifted(own[:, :HALO], "wide", -1)
    a0 = (24, 24, 256)
    (chunk,) = call(
        down0,
        (own, x_lo, x_hi),
        [(4, 25, 8, 128)],
        [a0] * 13 + [(24, 24, 128)],
        "down0",
        9,
        [HBM] * 3,
    )
    gathered = lax.all_to_all(chunk, "narrow", 0, 0)
    lo = shifted(gathered, "wide", 1)
    hi = shifted(gathered, "wide", -1)
    a1 = (28, 32, 128)
    to_up, to_down, mine, finer = call(
        down1,
        (lo, gathered, hi),
        [(14, 16, 128), (14, 16, 128), (24, 16, 128), (8, 128)],
        [a1] * 12 + [(24, 32, 256), (24, 32, 128), (4, 8, 128)],
        "down1",
        40,
        [HBM] * 3,
    )
    dn2 = shifted(to_up, "wide", 2)
    up2 = shifted(to_down, "wide", -2)
    dn4 = shifted(to_up, "wide", 4)
    up4 = shifted(to_down, "wide", -4)
    wide = lax.axis_size("wide")
    e2, sums = call(
        bottom,
        (dn4, dn2, mine, up2, up4, finer),
        [(8, 16, 128), (wide, 1, 128)],
        [(44, 16, 128)] * 9
        + [(22, 8, 128)] * 9
        + [(11, 8, 128)] * 9
        + [(40, 16, 128)] * 2
        + [(18, 8, 128)] * 2
        + [(5, 8, 128), (6, 16, 128)],
        "bottom",
    )
    every = lax.all_to_all(sums, "wide", 0, 0)
    out_s, out_c = call(
        up,
        (e2, lo, gathered, hi, own, x_lo, x_hi),
        [(16, 16, 256)] * 2,
        [a1] * 13
        + [a0] * 13
        + [(8, 32, 128), (8, 32, 256), (20, 48, 128), (20, 24, 128), (20, 24, 256)],
        "up",
        45,
        [VMEM] + [HBM] * 6,
    )
    return call(final, (every, out_s, out_c), [(16, 16, 256)], [], "final")[0]


def solution(mesh):
    spec = P("wide", "narrow", None)
    return jax.shard_map(
        per_device, mesh=mesh, in_specs=(spec, spec, spec), out_specs=spec, check_vma=False
    )
```

```python
import functools

import jax
import jax.numpy as jnp
from jax import lax
from jax.experimental import pallas as pl
from jax.experimental.pallas import tpu as pltpu
from jax.sharding import PartitionSpec as P

f32 = jnp.float32
HALO = 4
LIMIT = 24
C0, S0, W0, R0 = 22, 22, 20, 16
C1, S1, W1, R1 = 26, 26, 24, 8
C2, S2, W2, R2 = 42, 40, 38, 36
DAMPING = 0.8
BASE_TAU = 16.0
VMEM = pl.BlockSpec(memory_space=pltpu.VMEM)
HBM = pl.BlockSpec(memory_space=pltpu.HBM)


def half_tau(level):
    return 0.5 * BASE_TAU / 4.0**level


def iota(shape, dim):
    return lax.broadcasted_iota(jnp.int32, shape, dim)


def dot(x, matrix):
    matrix = matrix.astype(jnp.bfloat16)
    total = None
    for _ in range(3):
        part = x.astype(jnp.bfloat16)
        x = x - part.astype(f32)
        term = jnp.dot(part, matrix, preferred_element_type=f32)
        total = term if total is None else total + term
    return total


def rounded(x):
    return x.astype(jnp.bfloat16).astype(f32)


def ahead(x, axis):
    return pltpu.roll(x, x.shape[axis] - 1, axis)


def behind(x, axis):
    return pltpu.roll(x, 1, axis)


def at(i, n):
    return pl.ds(i, n) if n > 1 or not isinstance(i, int) else slice(i, i + 1)


def by_rows(lo, hi, n, fn, carry=None):
    count = (hi - lo) // n
    if count > 1:
        carry = lax.fori_loop(0, count, lambda t, c: fn(lo + t * n, n, c), carry)
    elif count == 1:
        carry = fn(lo, n, carry)
    rest = hi - lo - count * n
    if rest:
        carry = fn(lo + count * n, rest, carry)
    return carry


def coefficients(level, m, cx, cy, cz, dg, wt, lo, hi, n, y_len, z_len):
    tau = half_tau(level)
    cx[lo - 1] = rounded(tau * (m[lo - 1] + m[lo]))

    def body(i, n, carry):
        here = m[at(i, n)]
        shape = here.shape
        lane = lax.rem(iota(shape, 2), z_len)
        z_last = lane == z_len - 1
        z_first = lane == 0
        edge = rounded(tau * here)
        x_up = rounded(tau * (here + m[at(i + 1, n)]))
        cx[at(i, n)] = x_up
        y_up = rounded(tau * (here + ahead(here, 1)))
        if y_len is None:
            y_down = behind(y_up, 1)
            cy[at(i, n)] = y_up
        else:
            sub = iota(shape, 1)
            inner = jnp.where(sub >= y_len - 1, 0.0, y_up)
            y_up = jnp.where(sub == y_len - 1, edge, y_up)
            y_down = jnp.where(sub == 0, edge, behind(inner, 1))
            cy[at(i, n)] = inner
        inner = jnp.where(z_last, 0.0, rounded(tau * (here + ahead(here, 2))))
        cz[at(i, n)] = inner
        z_up = jnp.where(z_last, edge, inner)
        z_down = jnp.where(z_first, edge, behind(inner, 2))
        diagonal = 1.0 + x_up + cx[at(i - 1, n)] + y_up + y_down + z_up + z_down
        if dg is not None:
            dg[at(i, n)] = diagonal
        wt[at(i, n)] = jnp.where(here > 0.0, DAMPING / diagonal, 0.0)
        return carry

    by_rows(lo, hi, n, body, 0)


def coupled(i, n, v, cx, cy, cz):
    here = v[at(i, n)]
    up = cy[at(i, n)]
    side = cz[at(i, n)]
    total = cx[at(i, n)] * v[at(i + 1, n)] + cx[at(i - 1, n)] * v[at(i - 1, n)]
    total = total + (up * ahead(here, 1) + behind(up * here, 1))
    return total + (side * ahead(here, 2) + behind(side * here, 2))


def residual(i, n, r, v, cx, cy, cz, dg):
    return r - dg[at(i, n)] * v[at(i, n)] + coupled(i, n, v, cx, cy, cz)


def relaxed(i, n, r, v, wt, cx, cy, cz, *_):
    return (1.0 - DAMPING) * v[at(i, n)] + wt[at(i, n)] * (r[at(i, n)] + coupled(i, n, v, cx, cy, cz))


def start(lo, hi, n, source, out, wt):
    def body(i, n, carry):
        for s, o in zip(source, out):
            o[at(i, n)] = wt[at(i, n)] * s[at(i, n)]
        return carry

    by_rows(lo, hi, n, body, 0)


def sweep(lo, hi, n, source, v, out, coefs, wt):
    def body(i, n, carry):
        for s, a, o in zip(source, v, out):
            o[at(i, n)] = relaxed(i, n, s, a, wt, *coefs)
        return carry

    by_rows(lo, hi, n, body, 0)


def pairs(x):
    x = x.reshape(x.shape[0] // 2, 2, *x.shape[1:])
    return x[:, 0] + x[:, 1]


def doubled(x):
    x = jnp.broadcast_to(x[:, None], (x.shape[0], 2, *x.shape[1:]))
    return x.reshape(x.shape[0] * 2, *x.shape[2:])


def flat_dot(x, matrix):
    n = x.shape[0] * x.shape[1]
    return dot(x.reshape(n, x.shape[2]), matrix).reshape(x.shape[0], x.shape[1], matrix.shape[1])


def fold_y(ref, k, n, first, count):
    return ref[k : k + n, pl.ds(first, count, stride=2), :] + ref[k : k + n, pl.ds(first + 1, count, stride=2), :]


def coarse_z(z_in, lanes_in, z_out, lanes_out, fields):
    src = iota((lanes_in, lanes_out), 0)
    dst = iota((lanes_in, lanes_out), 1)
    target = lax.div(src, z_in) * z_out + lax.div(lax.rem(src, z_in), 2)
    return jnp.where((target == dst) & (src < fields * z_in), 0.125, 0.0).astype(f32)


def fine_z(z_in, lanes_in, z_out, lanes_out, fields):
    src = iota((lanes_in, lanes_out), 0)
    dst = iota((lanes_in, lanes_out), 1)
    wanted = lax.div(dst, z_out) * z_in + lax.div(lax.rem(dst, z_out), 2)
    return jnp.where((wanted == src) & (dst < fields * z_out), 1.0, 0.0).astype(f32)


def products(i, n, s, c, us, uc, coefs, sums):
    num, den = sums
    v_s, v_c = us[at(i, n)], uc[at(i, n)]
    r_s, r_c = s[at(i, n)], c[at(i, n)]
    res_s = residual(i, n, r_s, us, *coefs)
    res_c = residual(i, n, r_c, uc, *coefs)
    num = num + jnp.sum(v_s * r_c + res_s * v_c, axis=0)
    den = den + jnp.sum(v_s * r_s + res_s * v_s, axis=0)
    return res_s, res_c, (num, den)


def fetch(sources, targets, sems):
    copies = [pltpu.make_async_copy(a, b, sems.at[k]) for k, (a, b) in enumerate(zip(sources, targets))]
    for copy in copies:
        copy.start()
    return copies


def wait(copies):
    for copy in copies:
        copy.wait()


def sides(low, high):
    even = lax.rem(lax.axis_index("wide"), 2) == 0
    return jnp.where(even, high, low), jnp.where(even, low, high)


def fetch0(own, inner, outer, fields, sems):
    inner_at, outer_at = sides(0, 20)
    sources, targets = [], []
    for index, ref in enumerate(fields):
        for part, lo, n in ((own, 4, 16), (inner, inner_at, 4), (outer, outer_at, 4)):
            sources.append(part.at[index])
            targets.append(ref.at[pl.ds(lo, n)])
    return fetch(sources, targets, sems)


def fetch1(own, inner, outer, fields, sems):
    inner_at, outer_at = sides(2, 18)
    sources, targets = [], []
    for index, ref in fields:
        for source, lo in ((own, 10), (inner, inner_at), (outer, outer_at)):
            for j in range(4):
                sources.append(source.at[j, pl.ds(index * 8, 8)])
                targets.append(ref.at[pl.ds(lo, 8), pl.ds(8 * j, 8), :])
    return fetch(sources, targets, sems)


def down0(own, inner, outer, out, vs, vc, cx, cy, cz, dg, wt, ss, cc, m, us, uc, pair, thin, sems):
    copies = fetch0(own, inner, outer, (m, ss, cc), sems)
    wait(copies[:3])
    coefficients(0, m, cx, cy, cz, dg, wt, 1, 23, C0, None, 256)
    coefs = (cx, cy, cz, dg)
    wait(copies[3:])
    start(1, 23, S0, (ss, cc), (us, uc), wt)
    sweep(2, 22, W0, (ss, cc), (us, uc), (vs, vc), coefs, wt)

    def rest(i, n, sums):
        res_s, res_c, sums = products(i, n, ss, cc, vs, vc, coefs, sums)
        k = lax.div(i - 4, 2)
        pair[at(k, n // 2)] = pairs(res_s)
        pair[at(k + 8, n // 2)] = pairs(res_c)
        pair[at(k + 16, n // 2)] = pairs(m[at(i, n)])
        return sums

    zero = jnp.zeros((24, 256), f32)
    num, den = by_rows(4, 20, R0, rest, (zero, zero))
    thin[...] = flat_dot(pair[...], coarse_z(256, 256, 128, 128, 1))
    value = fold_y(thin, 0, 24, 4, 8)
    sub = iota((24, 256), 0)
    inside = (sub >= 4) & (sub < 20)
    num = jnp.sum(jnp.where(inside, num, 0.0))
    den = jnp.sum(jnp.where(inside, den, 0.0))
    lane = iota((8, 128), 1)
    both = jnp.where(lane == 0, num, jnp.where(lane == 1, den, 0.0))
    for j in range(4):
        out[j, 0:24] = value
        out[j, 24] = both


def down1(
    own, inner, outer, to_up, to_down, mine, sums,
    vs, vc, cx, cy, cz, dg, wt, ss, cc, m, us, uc, pair, thin, parts, sems,
):
    copies = fetch1(own, inner, outer, ((2, m), (0, ss), (1, cc)), sems)
    partial = fetch([own.at[j, 24] for j in range(4)], [parts.at[j] for j in range(4)], sems.at[pl.ds(36, 4)])
    for ref in (ss, cc, m, vs, vc):
        ref[0:2] = jnp.zeros((2, 32, 128), f32)
        ref[26:28] = jnp.zeros((2, 32, 128), f32)
    wait(copies[:12])
    coefficients(1, m, cx, cy, cz, dg, wt, 1, 27, C1, 32, 128)
    coefs = (cx, cy, cz, dg)
    wait(copies[12:])
    wait(partial)
    start(1, 27, S1, (ss, cc), (us, uc), wt)
    sweep(2, 26, W1, (ss, cc), (us, uc), (vs, vc), coefs, wt)

    def rest(i, n, sums):
        res_s, res_c, sums = products(i, n, ss, cc, vs, vc, coefs, sums)
        k = lax.div(i - 2, 2)
        pair[at(k, n // 2), :, 0:128] = pairs(res_s)
        pair[at(k, n // 2), :, 128:256] = pairs(res_c)
        both = pairs(m[at(i, n)])
        pair[at(k + 12, n // 2), :, 0:128] = both
        pair[at(k + 12, n // 2), :, 128:256] = both
        return sums

    zero = jnp.zeros((32, 128), f32)
    by_rows(2, 10, R1, rest, (zero, zero))
    num, den = by_rows(10, 18, R1, rest, (zero, zero))
    by_rows(18, 26, R1, rest, (zero, zero))
    thin[...] = flat_dot(pair[...], coarse_z(128, 256, 64, 128, 2))
    place = lax.axis_index("wide")
    low = jnp.where(place == 1, fold_y(thin, 0, 2, 0, 16), 0.0)
    mid = fold_y(thin, 2, 8, 0, 16)
    high = jnp.where(place == lax.axis_size("wide") - 2, fold_y(thin, 10, 2, 0, 16), 0.0)
    mob = fold_y(thin, 12, 12, 0, 16)
    mine[0:2] = low
    mine[2:10] = mid
    mine[10:12] = high
    mine[12:24] = mob
    to_up[0:2] = low
    to_up[2:10] = mid
    to_down[0:8] = mid
    to_down[8:10] = high
    left = iota((4, 16, 128), 2) < 64
    to_up[10:14] = jnp.where(left, mob[0:4], mob[4:8])
    to_down[10:14] = jnp.where(left, mob[4:8], mob[8:12])
    lane = iota((8, 128), 1)
    num = jnp.sum(num) * 8.0
    den = jnp.sum(den) * 8.0
    finer = parts[0] + parts[1] + parts[2] + parts[3]
    sums[...] = finer + jnp.where(lane == 0, num, jnp.where(lane == 1, den, 0.0))


def bottom(
    dn4, dn2, mine, up2, up4, finer, e2, sums,
    m2, r2, u2, v2, cx2, cy2, cz2, dg2, wt2,
    m3, r3, u3, v3, cx3, cy3, cz3, dg3, wt3,
    m4, r4, u4, v4, cx4, cy4, cz4, dg4, wt4,
    pair2, thin2, pair3, thin3, wide3, wide2,
):
    left = iota((4, 16, 128), 2) < 64

    def unpack(ref, first, r_at, m_at):
        r2[r_at : r_at + 8] = ref[first : first + 8]
        packed = ref[10:14]
        other = pltpu.roll(packed, 64, 2)
        m2[m_at : m_at + 4] = jnp.where(left, packed, other)
        m2[m_at + 4 : m_at + 8] = jnp.where(left, other, packed)

    unpack(dn4, 2, 2, 0)
    unpack(dn2, 2, 10, 8)
    unpack(up2, 0, 26, 28)
    unpack(up4, 0, 34, 36)
    r2[18:26] = mine[2:10]
    m2[16:28] = mine[12:24]
    r2[8:10] = r2[8:10] + dn2[0:2]
    r2[16:18] = r2[16:18] + mine[0:2]
    r2[26:28] = r2[26:28] + mine[10:12]
    r2[34:36] = r2[34:36] + up2[8:10]

    def both_products(r, v, res, z_len):
        num = v * pltpu.roll(r, 128 - z_len, 2)
        den = v * r
        if res is not None:
            num = num + res * pltpu.roll(v, 128 - z_len, 2)
            den = den + res * v
        mask = iota(v.shape, 2) < z_len
        return jnp.sum(jnp.where(mask, num, 0.0)), jnp.sum(jnp.where(mask, den, 0.0))

    c2 = (cx2, cy2, cz2, dg2)
    c3 = (cx3, cy3, cz3, dg3)
    c4 = (cx4, cy4, cz4, dg4)
    coefficients(2, m2, *c2, wt2, 1, 43, C2, 16, 64)
    start(2, 42, S2, (r2,), (u2,), wt2)
    sweep(3, 41, W2, (r2,), (u2,), (v2,), c2, wt2)

    def rest2(i, n, sums):
        res = residual(i, n, r2[at(i, n)], v2, *c2)
        pair2[at(lax.div(i - 4, 2), n // 2)] = pairs(res)
        return sums

    by_rows(4, 40, R2, rest2, 0)
    own = slice(20, 24)
    num2, den2 = both_products(r2[own], v2[own], residual(20, 4, r2[own], v2, *c2), 64)
    pair2[18:40] = pairs(m2[...])
    thin2[...] = flat_dot(pair2[...], coarse_z(64, 128, 32, 128, 2))
    r3[2:20] = fold_y(thin2, 0, 18, 0, 8)
    m3[...] = fold_y(thin2, 18, 22, 0, 8)

    coefficients(3, m3, *c3, wt3, 1, 21, 10, 8, 32)
    start(2, 20, 18, (r3,), (u3,), wt3)
    sweep(3, 19, 16, (r3,), (u3,), (v3,), c3, wt3)
    res = residual(4, 14, r3[4:18], v3, *c3)
    num3, den3 = both_products(r3[10:12], v3[10:12], res[6:8], 32)
    pair3[0:7] = pairs(res)
    pair3[7:18] = pairs(m3[...])
    thin3[...] = flat_dot(pair3[...], coarse_z(32, 128, 16, 128, 2))
    m4[...] = jnp.zeros((11, 8, 128), f32)
    r4[...] = jnp.zeros((11, 8, 128), f32)
    r4[2:9, 0:4, :] = fold_y(thin3, 0, 7, 0, 4)
    m4[:, 0:4, :] = fold_y(thin3, 7, 11, 0, 4)

    coefficients(4, m4, *c4, wt4, 1, 10, 9, 4, 16)
    start(2, 9, 7, (r4,), (u4,), wt4)
    sweep(3, 8, 5, (r4,), (u4,), (v4,), c4, wt4)
    num4, den4 = both_products(r4[5:6], v4[5:6], None, 16)
    num = 64.0 * num2 + 512.0 * num3 + 4096.0 * num4
    den = 64.0 * den2 + 512.0 * den3 + 4096.0 * den4
    lane = iota((8, 128), 1)
    total = finer[...] + jnp.where(lane == 0, num, jnp.where(lane == 1, den, 0.0))
    sums[...] = jnp.broadcast_to(total[0:1].reshape(1, 1, 128), sums.shape)

    wide3[:, pl.ds(0, 4, stride=2), :] = v4[3:8, 0:4, :]
    wide3[:, pl.ds(1, 4, stride=2), :] = v4[3:8, 0:4, :]
    v3[6:16] = v3[6:16] + doubled(flat_dot(wide3[...], fine_z(16, 128, 32, 128, 2)))
    sweep(7, 15, 8, (r3,), (v3,), (u3,), c3, wt3)
    sweep(8, 14, 6, (r3,), (u3,), (v3,), c3, wt3)
    wide2[:, pl.ds(0, 8, stride=2), :] = v3[8:14]
    wide2[:, pl.ds(1, 8, stride=2), :] = v3[8:14]
    v2[16:28] = v2[16:28] + doubled(flat_dot(wide2[...], fine_z(32, 128, 64, 128, 2)))
    sweep(17, 27, 10, (r2,), (v2,), (u2,), c2, wt2)
    e2[...] = relaxed(18, 8, r2, u2, wt2, *c2)


def up(
    e2, own1, inner1, outer1, own0, inner0, outer0, out_s, out_c,
    vs1, vc1, cx1, cy1, cz1, wt1, ss1, cc1, m1, as1, ac1, bs1, bc1,
    vs0, vc0, cx0, cy0, cz0, wt0, ss0, cc0, m0, as0, ac0, bs0, bc0,
    wide, add, block, thick, full, sems,
):
    copies1 = fetch1(own1, inner1, outer1, ((2, m1), (0, ss1), (1, cc1)), sems)
    copies0 = fetch0(own0, inner0, outer0, (m0, ss0, cc0), sems.at[pl.ds(36, 9)])
    c1 = (cx1, cy1, cz1)
    c0 = (cx0, cy0, cz0)
    wait(copies1)
    coefficients(1, m1, cx1, cy1, cz1, None, wt1, 5, 23, C1, 32, 128)
    start(5, 23, S1, (ss1, cc1), (as1, ac1), wt1)
    sweep(6, 22, W1, (ss1, cc1), (as1, ac1), (vs1, vc1), c1, wt1)
    wait(copies0)
    coefficients(0, m0, cx0, cy0, cz0, None, wt0, 1, 23, C0, None, 256)
    start(1, 23, S0, (ss0, cc0), (as0, ac0), wt0)
    sweep(2, 22, W0, (ss0, cc0), (as0, ac0), (vs0, vc0), c0, wt0)
    wide[:, pl.ds(0, 16, stride=2), :] = e2[...]
    wide[:, pl.ds(1, 16, stride=2), :] = e2[...]
    add[...] = flat_dot(wide[...], fine_z(64, 128, 128, 256, 2))

    def correct1(i, n, carry):
        k = lax.div(i - 6, 2)
        both = add[at(k, n // 2)]
        as1[at(i, n)] = vs1[at(i, n)] + doubled(both[:, :, 0:128])
        ac1[at(i, n)] = vc1[at(i, n)] + doubled(both[:, :, 128:256])
        return carry

    by_rows(6, 22, R1, correct1, 0)
    sweep(8, 20, W1, (ss1, cc1), (as1, ac1), (bs1, bc1), c1, wt1)
    place = lax.axis_index("narrow")
    block[:, 0:8, :] = jnp.zeros((20, 8, 128), f32)
    block[:, 40:48, :] = jnp.zeros((20, 8, 128), f32)

    def last1(i, n, carry):
        for index, (r, v) in enumerate(((ss1, bs1), (cc1, bc1))):
            value = relaxed(i, n, r, v, wt1, *c1)
            block[at(index * 10 + i - 9, n), 8:40, :] = value
        return carry

    by_rows(9, 19, 5, last1, 0)
    value = block[:, pl.ds(pl.multiple_of(8 * place, 8), 24), :][:, 6:18, :]
    thick[:, pl.ds(0, 12, stride=2), :] = value
    thick[:, pl.ds(1, 12, stride=2), :] = value
    full[...] = flat_dot(thick[...], fine_z(128, 128, 256, 256, 1))

    def correct0(i, n, carry):
        k = lax.div(i - 2, 2)
        as0[at(i, n)] = vs0[at(i, n)] + doubled(full[at(k, n // 2)])
        ac0[at(i, n)] = vc0[at(i, n)] + doubled(full[at(10 + k, n // 2)])
        return carry

    by_rows(2, 22, R0, correct0, 0)
    sweep(3, 21, W0, (ss0, cc0), (as0, ac0), (bs0, bc0), c0, wt0)

    def last0(i, n, carry):
        for r, v, o in ((ss0, bs0, out_s), (cc0, bc0, out_c)):
            o[at(i - 4, n)] = relaxed(i, n, r, v, wt0, *c0)[:, 4:20, :]
        return carry

    by_rows(4, 20, W0, last0, 0)


def final(every, out_s, out_c, out):
    total = jnp.sum(every[...], axis=0)
    lane = iota((1, 128), 1)
    num = jnp.sum(jnp.where(lane == 0, total, 0.0), axis=1, keepdims=True)
    den = jnp.sum(jnp.where(lane == 1, total, 0.0), axis=1, keepdims=True)
    ratio = (num / (1.0 + den))[0, 0]
    out[...] = out_c[...] - ratio * out_s[...]


def call(kernel, ins, outs, scratch, name, sems=0, specs=None):
    scratch = [pltpu.VMEM(s, f32) for s in scratch]
    if sems:
        scratch.append(pltpu.SemaphoreType.DMA((sems,)))
    return pl.pallas_call(
        kernel,
        out_shape=[jax.ShapeDtypeStruct(s, f32) for s in outs],
        in_specs=specs or [VMEM] * len(ins),
        out_specs=[VMEM] * len(outs),
        scratch_shapes=scratch,
        compiler_params=pltpu.CompilerParams(vmem_limit_bytes=LIMIT * 2**20),
        name=name,
    )(*ins)


def shifted(value, axis, by):
    size = lax.axis_size(axis)
    return lax.ppermute(value, axis, [(i, i + by) for i in range(size) if 0 <= i + by < size])


def swapped(value, first):
    pairs = [(i, i + 1) for i in range(first, lax.axis_size("wide") - 1, 2)]
    return lax.ppermute(value, "wide", pairs + [(b, a) for a, b in pairs])


def per_device(mobility, sav_vector, cotangent):
    own = jnp.stack([mobility, sav_vector, cotangent])
    y_lo = shifted(own[:, :, -HALO:], "narrow", 1)
    y_hi = shifted(own[:, :, :HALO], "narrow", -1)
    own = jnp.concatenate([y_lo, own, y_hi], axis=2)
    last = own.shape[1] - HALO
    odd = lax.rem(lax.axis_index("wide"), 2)
    x_outer = swapped(lax.dynamic_slice_in_dim(own, odd * last, HALO, axis=1), 1)
    x_inner = swapped(lax.dynamic_slice_in_dim(own, (1 - odd) * last, HALO, axis=1), 0)
    a0 = (24, 24, 256)
    (chunk,) = call(
        down0,
        (own, x_inner, x_outer),
        [(4, 25, 8, 128)],
        [a0] * 13 + [(24, 24, 128)],
        "down0",
        9,
        [HBM] * 3,
    )
    gathered = lax.all_to_all(chunk, "narrow", 0, 0)
    outer = swapped(gathered, 1)
    inner = swapped(gathered, 0)
    a1 = (28, 32, 128)
    to_up, to_down, mine, finer = call(
        down1,
        (gathered, inner, outer),
        [(14, 16, 128), (14, 16, 128), (24, 16, 128), (8, 128)],
        [a1] * 12 + [(24, 32, 256), (24, 32, 128), (4, 8, 128)],
        "down1",
        40,
        [HBM] * 3,
    )
    dn2 = shifted(to_up, "wide", 2)
    up2 = shifted(to_down, "wide", -2)
    dn4 = shifted(to_up, "wide", 4)
    up4 = shifted(to_down, "wide", -4)
    wide = lax.axis_size("wide")
    e2, sums = call(
        bottom,
        (dn4, dn2, mine, up2, up4, finer),
        [(8, 16, 128), (wide, 1, 128)],
        [(44, 16, 128)] * 9
        + [(22, 8, 128)] * 9
        + [(11, 8, 128)] * 9
        + [(40, 16, 128)] * 2
        + [(18, 8, 128)] * 2
        + [(5, 8, 128), (6, 16, 128)],
        "bottom",
    )
    every = lax.all_to_all(sums, "wide", 0, 0)
    out_s, out_c = call(
        up,
        (e2, gathered, inner, outer, own, x_inner, x_outer),
        [(16, 16, 256)] * 2,
        [a1] * 13
        + [a0] * 13
        + [(8, 32, 128), (8, 32, 256), (20, 48, 128), (20, 24, 128), (20, 24, 256)],
        "up",
        45,
        [VMEM] + [HBM] * 6,
    )
    return call(final, (every, out_s, out_c), [(16, 16, 256)], [], "final")[0]


def solution(mesh):
    spec = P("wide", "narrow", None)
    return jax.shard_map(
        per_device, mesh=mesh, in_specs=(spec, spec, spec), out_specs=spec, check_vma=False
    )
```

```python
import functools

import jax
import jax.numpy as jnp
from jax import lax
from jax.experimental import pallas as pl
from jax.experimental.pallas import tpu as pltpu
from jax.sharding import PartitionSpec as P

f32 = jnp.float32
HALO = 4
LIMIT = 24
ROOM = 6144
C0, S0, W0, R0 = 22, 22, 20, 16
C1, S1, W1, R1 = 26, 26, 24, 8
C2, S2, W2, R2 = 42, 40, 38, 36
DAMPING = 0.8
BASE_TAU = 16.0
VMEM = pl.BlockSpec(memory_space=pltpu.VMEM)
HBM = pl.BlockSpec(memory_space=pltpu.HBM)


def half_tau(level):
    return 0.5 * BASE_TAU / 4.0**level


def iota(shape, dim):
    return lax.broadcasted_iota(jnp.int32, shape, dim)


def dot(x, matrix):
    matrix = matrix.astype(jnp.bfloat16)
    total = None
    for _ in range(3):
        part = x.astype(jnp.bfloat16)
        x = x - part.astype(f32)
        term = jnp.dot(part, matrix, preferred_element_type=f32)
        total = term if total is None else total + term
    return total


def rounded(x):
    return x.astype(jnp.bfloat16).astype(f32)


def ahead(x, axis):
    return pltpu.roll(x, x.shape[axis] - 1, axis)


def behind(x, axis):
    return pltpu.roll(x, 1, axis)


def at(i, n):
    return pl.ds(i, n) if n > 1 or not isinstance(i, int) else slice(i, i + 1)


def by_rows(lo, hi, n, fn, carry=None):
    count = (hi - lo) // n
    if count > 1:
        carry = lax.fori_loop(0, count, lambda t, c: fn(lo + t * n, n, c), carry)
    elif count == 1:
        carry = fn(lo, n, carry)
    rest = hi - lo - count * n
    if rest:
        carry = fn(lo + count * n, rest, carry)
    return carry


def coefficients(level, m, cx, cy, cz, dg, wt, lo, hi, n, y_len, z_len):
    tau = half_tau(level)
    cx[lo - 1] = rounded(tau * (m[lo - 1] + m[lo]))

    def body(i, n, carry):
        here = m[at(i, n)]
        shape = here.shape
        lane = lax.rem(iota(shape, 2), z_len)
        z_last = lane == z_len - 1
        z_first = lane == 0
        edge = rounded(tau * here)
        x_up = rounded(tau * (here + m[at(i + 1, n)]))
        cx[at(i, n)] = x_up
        y_up = rounded(tau * (here + ahead(here, 1)))
        if y_len is None:
            y_down = behind(y_up, 1)
            cy[at(i, n)] = y_up
        else:
            sub = iota(shape, 1)
            inner = jnp.where(sub >= y_len - 1, 0.0, y_up)
            y_up = jnp.where(sub == y_len - 1, edge, y_up)
            y_down = jnp.where(sub == 0, edge, behind(inner, 1))
            cy[at(i, n)] = inner
        inner = jnp.where(z_last, 0.0, rounded(tau * (here + ahead(here, 2))))
        cz[at(i, n)] = inner
        z_up = jnp.where(z_last, edge, inner)
        z_down = jnp.where(z_first, edge, behind(inner, 2))
        diagonal = 1.0 + x_up + cx[at(i - 1, n)] + y_up + y_down + z_up + z_down
        if dg is not None:
            dg[at(i, n)] = diagonal
        wt[at(i, n)] = jnp.where(here > 0.0, DAMPING / diagonal, 0.0)
        return carry

    by_rows(lo, hi, n, body, 0)


def coupled(i, n, v, cx, cy, cz):
    here = v[at(i, n)]
    up = cy[at(i, n)]
    side = cz[at(i, n)]
    total = cx[at(i, n)] * v[at(i + 1, n)] + cx[at(i - 1, n)] * v[at(i - 1, n)]
    total = total + (up * ahead(here, 1) + behind(up * here, 1))
    return total + (side * ahead(here, 2) + behind(side * here, 2))


def residual(i, n, r, v, cx, cy, cz, dg):
    return r - dg[at(i, n)] * v[at(i, n)] + coupled(i, n, v, cx, cy, cz)


def relaxed(i, n, r, v, wt, cx, cy, cz, *_):
    return (1.0 - DAMPING) * v[at(i, n)] + wt[at(i, n)] * (r[at(i, n)] + coupled(i, n, v, cx, cy, cz))


def start(lo, hi, n, source, out, wt):
    def body(i, n, carry):
        for s, o in zip(source, out):
            o[at(i, n)] = wt[at(i, n)] * s[at(i, n)]
        return carry

    by_rows(lo, hi, n, body, 0)


def sweep(lo, hi, n, source, v, out, coefs, wt):
    def body(i, n, carry):
        for s, a, o in zip(source, v, out):
            o[at(i, n)] = relaxed(i, n, s, a, wt, *coefs)
        return carry

    by_rows(lo, hi, n, body, 0)


def pairs(x):
    x = x.reshape(x.shape[0] // 2, 2, *x.shape[1:])
    return x[:, 0] + x[:, 1]


def doubled(x):
    x = jnp.broadcast_to(x[:, None], (x.shape[0], 2, *x.shape[1:]))
    return x.reshape(x.shape[0] * 2, *x.shape[2:])


def flat_dot(x, matrix):
    n = x.shape[0] * x.shape[1]
    return dot(x.reshape(n, x.shape[2]), matrix).reshape(x.shape[0], x.shape[1], matrix.shape[1])


def fold_y(ref, k, n, first, count):
    return ref[k : k + n, pl.ds(first, count, stride=2), :] + ref[k : k + n, pl.ds(first + 1, count, stride=2), :]


def coarse_z(z_in, lanes_in, z_out, lanes_out, fields):
    src = iota((lanes_in, lanes_out), 0)
    dst = iota((lanes_in, lanes_out), 1)
    target = lax.div(src, z_in) * z_out + lax.div(lax.rem(src, z_in), 2)
    return jnp.where((target == dst) & (src < fields * z_in), 0.125, 0.0).astype(f32)


def fine_z(z_in, lanes_in, z_out, lanes_out, fields):
    src = iota((lanes_in, lanes_out), 0)
    dst = iota((lanes_in, lanes_out), 1)
    wanted = lax.div(dst, z_out) * z_in + lax.div(lax.rem(dst, z_out), 2)
    return jnp.where((wanted == src) & (dst < fields * z_out), 1.0, 0.0).astype(f32)


def products(i, n, s, c, us, uc, coefs, sums):
    num, den = sums
    v_s, v_c = us[at(i, n)], uc[at(i, n)]
    r_s, r_c = s[at(i, n)], c[at(i, n)]
    res_s = residual(i, n, r_s, us, *coefs)
    res_c = residual(i, n, r_c, uc, *coefs)
    num = num + jnp.sum(v_s * r_c + res_s * v_c, axis=0)
    den = den + jnp.sum(v_s * r_s + res_s * v_s, axis=0)
    return res_s, res_c, (num, den)


def fetch(sources, targets, sems):
    copies = [pltpu.make_async_copy(a, b, sems.at[k]) for k, (a, b) in enumerate(zip(sources, targets))]
    for copy in copies:
        copy.start()
    return copies


def wait(copies):
    for copy in copies:
        copy.wait()


def sides(low, high):
    even = lax.rem(lax.axis_index("wide"), 2) == 0
    return jnp.where(even, high, low), jnp.where(even, low, high)


def fetch0(own, inner, outer, fields, sems):
    inner_at, outer_at = sides(0, 20)
    sources, targets = [], []
    for index, ref in enumerate(fields):
        for part, lo, n in ((own, 4, 16), (inner, inner_at, 4), (outer, outer_at, 4)):
            sources.append(part.at[index])
            targets.append(ref.at[pl.ds(lo, n)])
    return fetch(sources, targets, sems)


def fetch1(own, inner, outer, fields, sems):
    inner_at, outer_at = sides(2, 18)
    sources, targets = [], []
    for index, ref in fields:
        for source, lo in ((own, 10), (inner, inner_at), (outer, outer_at)):
            for j in range(4):
                sources.append(source.at[j, pl.ds(index * 8, 8)])
                targets.append(ref.at[pl.ds(lo, 8), pl.ds(8 * j, 8), :])
    return fetch(sources, targets, sems)


def down0(own, inner, outer, out, vs, vc, cx, cy, cz, dg, wt, ss, cc, m, us, uc, pair, thin, sems):
    copies = fetch0(own, inner, outer, (m, ss, cc), sems)
    wait(copies[:3])
    coefficients(0, m, cx, cy, cz, dg, wt, 1, 23, C0, None, 256)
    coefs = (cx, cy, cz, dg)
    wait(copies[3:])
    start(1, 23, S0, (ss, cc), (us, uc), wt)
    sweep(2, 22, W0, (ss, cc), (us, uc), (vs, vc), coefs, wt)

    def rest(i, n, sums):
        res_s, res_c, sums = products(i, n, ss, cc, vs, vc, coefs, sums)
        k = lax.div(i - 4, 2)
        pair[at(k, n // 2)] = pairs(res_s)
        pair[at(k + 8, n // 2)] = pairs(res_c)
        pair[at(k + 16, n // 2)] = pairs(m[at(i, n)])
        return sums

    zero = jnp.zeros((24, 256), f32)
    num, den = by_rows(4, 20, R0, rest, (zero, zero))
    thin[...] = flat_dot(pair[...], coarse_z(256, 256, 128, 128, 1))
    value = fold_y(thin, 0, 24, 4, 8)
    sub = iota((24, 256), 0)
    inside = (sub >= 4) & (sub < 20)
    num = jnp.sum(jnp.where(inside, num, 0.0))
    den = jnp.sum(jnp.where(inside, den, 0.0))
    lane = iota((8, 128), 1)
    both = jnp.where(lane == 0, num, jnp.where(lane == 1, den, 0.0))
    for j in range(4):
        out[j, 0:24] = value
        out[j, 24] = both


def down1(
    own, inner, outer, piece, mine,
    vs, vc, cx, cy, cz, dg, wt, ss, cc, m, us, uc, pair, thin, parts, sems,
):
    copies = fetch1(own, inner, outer, ((2, m), (0, ss), (1, cc)), sems)
    partial = fetch([own.at[j, 24] for j in range(4)], [parts.at[j] for j in range(4)], sems.at[pl.ds(36, 4)])
    wait(copies[:12])
    coefficients(1, m, cx, cy, cz, dg, wt, 3, 25, C1, 32, 128)
    coefs = (cx, cy, cz, dg)
    wait(copies[12:])
    wait(partial)
    start(3, 25, S1, (ss, cc), (us, uc), wt)
    sweep(4, 24, W1, (ss, cc), (us, uc), (vs, vc), coefs, wt)

    def rest(i, n, sums):
        res_s, res_c, sums = products(i, n, ss, cc, vs, vc, coefs, sums)
        k = (i - 6) // 2
        pair[at(k, n // 2), :, 0:128] = pairs(res_s)
        pair[at(k, n // 2), :, 128:256] = pairs(res_c)
        return sums

    zero = jnp.zeros((32, 128), f32)
    rest(6, 4, (zero, zero))
    num, den = rest(10, 8, (zero, zero))
    rest(18, 4, (zero, zero))
    both = pairs(m[2:26])
    pair[8:20, :, 0:128] = both
    pair[8:20, :, 128:256] = both
    thin[...] = flat_dot(pair[...], coarse_z(128, 256, 64, 128, 2))
    mid = fold_y(thin, 0, 8, 0, 16)
    mob = fold_y(thin, 8, 12, 0, 16)
    even = lax.rem(lax.axis_index("wide"), 2) == 0
    mine[0:8] = mid
    mine[8:20] = mob
    piece[0:8] = mid
    left = iota((4, 16, 128), 2) < 64
    piece[8:12] = jnp.where(
        left, jnp.where(even, mob[0:4], mob[4:8]), jnp.where(even, mob[4:8], mob[8:12])
    )
    lane = iota((8, 128), 1)
    num = jnp.sum(num) * 8.0
    den = jnp.sum(den) * 8.0
    finer = parts[0] + parts[1] + parts[2] + parts[3]
    total = finer + jnp.where(lane == 0, num, jnp.where(lane == 1, den, 0.0))
    for ref, row in ((piece, 12), (mine, 20)):
        ref[row] = jnp.concatenate([total, total], axis=0)


def bottom(
    mine, near, far, pair_own, pair_near, pair_far, e2_out, sums,
    m2, r2, u2, v2, cx2, cy2, cz2, dg2, wt2,
    m3, r3, u3, v3, cx3, cy3, cz3, dg3, wt3,
    m4, r4, u4, v4, cx4, cy4, cz4, dg4, wt4,
    pair2, thin2, pair3, thin3, wide3, wide2, e2, sems,
):
    left = iota((4, 16, 128), 2) < 64
    place = lax.axis_index("wide")
    size = lax.axis_size("wide")

    even = lax.rem(place, 2) == 0

    def choose(a, b):
        return jnp.where(even, a, b)

    def held(distance, value):
        return jnp.where((place + distance >= 0) & (place + distance < size), value, 0.0)

    def unpack(ref, distance):
        packed = held(distance, ref[8:12])
        other = pltpu.roll(packed, 64, 2)
        return held(distance, ref[0:8]), jnp.where(left, packed, other), jnp.where(left, other, packed)

    r2[18:26] = mine[0:8]
    m2[16:28] = mine[8:20]
    for ref, distance, r_at, m_at in (
        (near, choose(-2, 2), choose(10, 26), choose(8, 28)),
        (far, choose(-4, 4), choose(2, 34), choose(0, 36)),
        (pair_near, choose(3, -3), choose(30, 6), choose(32, 4)),
    ):
        cells, m_low, m_high = unpack(ref, distance)
        r2[pl.ds(r_at, 8)] = cells
        m2[pl.ds(m_at, 4)] = m_low
        m2[pl.ds(m_at + 4, 4)] = m_high
    cells, m_low, m_high = unpack(pair_own, 0)
    r2[pl.ds(choose(26, 14), 4)] = choose(cells[4:8], cells[0:4])
    m2[pl.ds(choose(28, 12), 4)] = choose(m_high, m_low)
    cells, m_low, m_high = unpack(pair_far, choose(5, -5))
    r2[pl.ds(choose(38, 2), 4)] = choose(cells[0:4], cells[4:8])
    m2[pl.ds(choose(40, 0), 4)] = choose(m_low, m_high)

    lo = jnp.where(even, jnp.where(place == 2, -2, 0), jnp.where(place == 3, -3, -2))
    hi = jnp.where(place == size - 4, 3, 2)

    def both_products(r, v, res, z_len, rows):
        num = v * pltpu.roll(r, 128 - z_len, 2)
        den = v * r
        if res is not None:
            num = num + res * pltpu.roll(v, 128 - z_len, 2)
            den = den + res * v
        device = lax.div(iota(v.shape, 0), rows) - 3
        mask = (iota(v.shape, 2) < z_len) & (device >= lo) & (device <= hi)
        num = jnp.sum(jnp.where(mask, num, 0.0), axis=0)
        den = jnp.sum(jnp.where(mask, den, 0.0), axis=0)
        return num, den

    c2 = (cx2, cy2, cz2, dg2)
    c3 = (cx3, cy3, cz3, dg3)
    c4 = (cx4, cy4, cz4, dg4)
    coefficients(2, m2, *c2, wt2, 1, 43, C2, 16, 64)
    start(2, 42, S2, (r2,), (u2,), wt2)
    sweep(3, 41, W2, (r2,), (u2,), (v2,), c2, wt2)

    res = residual(4, 36, r2[4:40], v2, *c2)
    pair2[0:18] = pairs(res)
    kept = slice(8, 36)
    num2, den2 = both_products(r2[kept], v2[kept], res[4:32], 64, 4)
    pair2[18:40] = pairs(m2[...])
    thin2[...] = flat_dot(pair2[...], coarse_z(64, 128, 32, 128, 2))
    r3[2:20] = fold_y(thin2, 0, 18, 0, 8)
    m3[...] = fold_y(thin2, 18, 22, 0, 8)

    coefficients(3, m3, *c3, wt3, 1, 21, 10, 8, 32)
    start(2, 20, 18, (r3,), (u3,), wt3)
    sweep(3, 19, 16, (r3,), (u3,), (v3,), c3, wt3)
    res = residual(4, 14, r3[4:18], v3, *c3)
    kept = slice(4, 18)
    num3, den3 = both_products(r3[kept], v3[kept], res, 32, 2)
    pair3[0:7] = pairs(res)
    pair3[7:18] = pairs(m3[...])
    thin3[...] = flat_dot(pair3[...], coarse_z(32, 128, 16, 128, 2))
    m4[...] = jnp.zeros((11, 8, 128), f32)
    r4[...] = jnp.zeros((11, 8, 128), f32)
    r4[2:9, 0:4, :] = fold_y(thin3, 0, 7, 0, 4)
    m4[:, 0:4, :] = fold_y(thin3, 7, 11, 0, 4)

    coefficients(4, m4, *c4, wt4, 1, 10, 9, 4, 16)
    u4[1] = jnp.zeros((8, 128), f32)
    u4[9] = jnp.zeros((8, 128), f32)
    start(2, 9, 7, (r4,), (u4,), wt4)
    sweep(2, 9, 7, (r4,), (u4,), (v4,), c4, wt4)
    wide3[:, pl.ds(0, 4, stride=2), :] = v4[3:8, 0:4, :]
    wide3[:, pl.ds(1, 4, stride=2), :] = v4[3:8, 0:4, :]
    v3[6:16] = v3[6:16] + doubled(flat_dot(wide3[...], fine_z(16, 128, 32, 128, 2)))
    sweep(7, 15, 8, (r3,), (v3,), (u3,), c3, wt3)
    sweep(8, 14, 6, (r3,), (u3,), (v3,), c3, wt3)
    wide2[:, pl.ds(0, 8, stride=2), :] = v3[8:14]
    wide2[:, pl.ds(1, 8, stride=2), :] = v3[8:14]
    v2[16:28] = v2[16:28] + doubled(flat_dot(wide2[...], fine_z(32, 128, 64, 128, 2)))
    sweep(17, 27, 10, (r2,), (v2,), (u2,), c2, wt2)
    e2[...] = relaxed(18, 8, r2, u2, wt2, *c2)
    copies = fetch([e2], [e2_out.at[pl.ds(0, 8)]], sems)
    kept = slice(2, 9)
    num4, den4 = both_products(r4[kept], v4[kept], None, 16, 1)
    num = 64.0 * jnp.sum(num2) + 512.0 * jnp.sum(num3) + 4096.0 * jnp.sum(num4)
    den = 64.0 * jnp.sum(den2) + 512.0 * jnp.sum(den3) + 4096.0 * jnp.sum(den4)
    lane = iota((8, 128), 1)
    finer = mine[20, 0:8] + near[12, 0:8] + pair_own[12, 0:8] + pair_near[12, 0:8]
    total = finer + jnp.where(lane == 0, num, jnp.where(lane == 1, den, 0.0))
    sums[...] = jnp.broadcast_to(total[0:1].reshape(1, 1, 128), sums.shape)
    wait(copies)


def up(
    e2_in, own1, inner1, outer1, own0, inner0, outer0, out_s, out_c,
    vs1, vc1, cx1, cy1, cz1, wt1, ss1, cc1, m1, as1, ac1, bs1, bc1,
    vs0, vc0, cx0, cy0, cz0, wt0, ss0, cc0, m0, as0, ac0, bs0, bc0,
    wide, add, block, thick, full, e2, sems,
):
    copies1 = fetch1(own1, inner1, outer1, ((2, m1), (0, ss1), (1, cc1)), sems)
    copies0 = fetch0(own0, inner0, outer0, (m0, ss0, cc0), sems.at[pl.ds(36, 9)])
    copies2 = fetch([e2_in.at[pl.ds(0, 8)]], [e2], sems.at[pl.ds(45, 1)])
    c1 = (cx1, cy1, cz1)
    c0 = (cx0, cy0, cz0)
    wait(copies1)
    coefficients(1, m1, cx1, cy1, cz1, None, wt1, 5, 23, C1, 32, 128)
    start(5, 23, S1, (ss1, cc1), (as1, ac1), wt1)
    sweep(6, 22, W1, (ss1, cc1), (as1, ac1), (vs1, vc1), c1, wt1)
    wait(copies0)
    coefficients(0, m0, cx0, cy0, cz0, None, wt0, 1, 23, C0, None, 256)
    start(1, 23, S0, (ss0, cc0), (as0, ac0), wt0)
    sweep(2, 22, W0, (ss0, cc0), (as0, ac0), (vs0, vc0), c0, wt0)
    wait(copies2)
    wide[:, pl.ds(0, 16, stride=2), :] = e2[...]
    wide[:, pl.ds(1, 16, stride=2), :] = e2[...]
    add[...] = flat_dot(wide[...], fine_z(64, 128, 128, 256, 2))

    def correct1(i, n, carry):
        k = lax.div(i - 6, 2)
        both = add[at(k, n // 2)]
        as1[at(i, n)] = vs1[at(i, n)] + doubled(both[:, :, 0:128])
        ac1[at(i, n)] = vc1[at(i, n)] + doubled(both[:, :, 128:256])
        return carry

    by_rows(6, 22, R1, correct1, 0)
    sweep(8, 20, W1, (ss1, cc1), (as1, ac1), (bs1, bc1), c1, wt1)
    place = lax.axis_index("narrow")
    block[:, 0:8, :] = jnp.zeros((20, 8, 128), f32)
    block[:, 40:48, :] = jnp.zeros((20, 8, 128), f32)

    def last1(i, n, carry):
        for index, (r, v) in enumerate(((ss1, bs1), (cc1, bc1))):
            value = relaxed(i, n, r, v, wt1, *c1)
            block[at(index * 10 + i - 9, n), 8:40, :] = value
        return carry

    by_rows(9, 19, 5, last1, 0)
    value = block[:, pl.ds(pl.multiple_of(8 * place, 8), 24), :][:, 6:18, :]
    thick[:, pl.ds(0, 12, stride=2), :] = value
    thick[:, pl.ds(1, 12, stride=2), :] = value
    full[...] = flat_dot(thick[...], fine_z(128, 128, 256, 256, 1))

    def correct0(i, n, carry):
        k = lax.div(i - 2, 2)
        as0[at(i, n)] = vs0[at(i, n)] + doubled(full[at(k, n // 2)])
        ac0[at(i, n)] = vc0[at(i, n)] + doubled(full[at(10 + k, n // 2)])
        return carry

    by_rows(2, 22, R0, correct0, 0)
    sweep(3, 21, W0, (ss0, cc0), (as0, ac0), (bs0, bc0), c0, wt0)

    def last0(i, n, carry):
        for r, v, o in ((ss0, bs0, out_s), (cc0, bc0, out_c)):
            o[at(i - 4, n)] = relaxed(i, n, r, v, wt0, *c0)[:, 4:20, :]
        return carry

    by_rows(4, 20, W0, last0, 0)


def final(every, out_s, out_c, out, held, sems):
    total = jnp.sum(every[...], axis=0)
    lane = iota((1, 128), 1)
    num = jnp.sum(jnp.where(lane == 0, total, 0.0), axis=1, keepdims=True)
    den = jnp.sum(jnp.where(lane == 1, total, 0.0), axis=1, keepdims=True)
    ratio = (num / (1.0 + den))[0, 0]
    copies = []
    for k in range(4):
        rows = pl.ds(4 * k, 4)
        held[rows] = out_c[rows] - ratio * out_s[rows]
        copies += fetch([held.at[rows]], [out.at[rows]], sems.at[pl.ds(k, 1)])
    wait(copies)


def call(kernel, ins, outs, scratch, name, sems=0, specs=None, out_specs=None):
    scratch = [pltpu.VMEM(s, f32) for s in scratch]
    if sems:
        scratch.append(pltpu.SemaphoreType.DMA((sems,)))
    return pl.pallas_call(
        kernel,
        out_shape=[jax.ShapeDtypeStruct(s, f32) for s in outs],
        in_specs=specs or [VMEM] * len(ins),
        out_specs=out_specs or [VMEM] * len(outs),
        scratch_shapes=scratch,
        compiler_params=pltpu.CompilerParams(vmem_limit_bytes=LIMIT * 2**20),
        name=name,
    )(*ins)


def shifted(value, axis, by):
    size = lax.axis_size(axis)
    return lax.ppermute(value, axis, [(i, i + by) for i in range(size) if 0 <= i + by < size])


def apart(value, by):
    size = lax.axis_size("wide")
    return lax.ppermute(value, "wide", [(i, (i + by * (1 - 2 * (i % 2))) % size) for i in range(size)])


def swapped(value, first):
    pairs = [(i, i + 1) for i in range(first, lax.axis_size("wide") - 1, 2)]
    return lax.ppermute(value, "wide", pairs + [(b, a) for a, b in pairs])


def per_device(mobility, sav_vector, cotangent):
    own = jnp.stack([mobility, sav_vector, cotangent])
    y_lo = shifted(own[:, :, -HALO:], "narrow", 1)
    y_hi = shifted(own[:, :, :HALO], "narrow", -1)
    own = jnp.concatenate([y_lo, own, y_hi], axis=2)
    last = own.shape[1] - HALO
    odd = lax.rem(lax.axis_index("wide"), 2)
    x_outer = swapped(lax.dynamic_slice_in_dim(own, odd * last, HALO, axis=1), 1)
    x_inner = swapped(lax.dynamic_slice_in_dim(own, (1 - odd) * last, HALO, axis=1), 0)
    a0 = (24, 24, 256)
    (chunk,) = call(
        down0,
        (own, x_inner, x_outer),
        [(4, 25, 8, 128)],
        [a0] * 13 + [(24, 24, 128)],
        "down0",
        9,
        [HBM] * 3,
    )
    gathered = lax.all_to_all(chunk, "narrow", 0, 0)
    outer = swapped(gathered, 1)
    inner = swapped(gathered, 0)
    a1 = (28, 32, 128)
    piece, mine = call(
        down1,
        (gathered, inner, outer),
        [(13, 16, 128), (21, 16, 128)],
        [a1] * 12 + [(20, 32, 256), (20, 32, 128), (4, 8, 128)],
        "down1",
        40,
        [HBM] * 3,
    )
    near = apart(piece, 2)
    far = apart(piece, 4)
    pair_own = swapped(piece, 0)
    pair_near = swapped(near, 0)
    pair_far = swapped(far, 0)
    wide = lax.axis_size("wide")
    e2, sums = call(
        bottom,
        (mine, near, far, pair_own, pair_near, pair_far),
        [(ROOM, 16, 128), (wide // 4, 1, 128)],
        [(44, 16, 128)] * 9
        + [(22, 8, 128)] * 9
        + [(11, 8, 128)] * 9
        + [(40, 16, 128)] * 2
        + [(18, 8, 128)] * 2
        + [(5, 8, 128), (6, 16, 128), (8, 16, 128)],
        "bottom",
        1,
        None,
        [HBM, VMEM],
    )
    groups = [[i for i in range(wide) if (i // 2 + 2 * (i % 2)) % 4 == s] for s in range(4)]
    every = lax.all_to_all(sums, "wide", 0, 0, axis_index_groups=groups)
    out_s, out_c = call(
        up,
        (e2, gathered, inner, outer, own, x_inner, x_outer),
        [(16, 16, 256)] * 2,
        [a1] * 13
        + [a0] * 13
        + [(8, 32, 128), (8, 32, 256), (20, 48, 128), (20, 24, 128), (20, 24, 256), (8, 16, 128)],
        "up",
        46,
        [HBM] * 7,
    )
    return call(final, (every, out_s, out_c), [(16, 16, 256)], [(16, 16, 256)], "final", 4, None, [HBM])[0]


def solution(mesh):
    spec = P("wide", "narrow", None)
    return jax.shard_map(
        per_device, mesh=mesh, in_specs=(spec, spec, spec), out_specs=spec, check_vma=False
    )
```

```python
import functools

import jax
import jax.numpy as jnp
from jax import lax
from jax.experimental import pallas as pl
from jax.experimental.pallas import tpu as pltpu
from jax.sharding import PartitionSpec as P

f32 = jnp.float32
HALO = 4
LIMIT = 24
ROOM = 6144
C0, S0, W0, R0 = 22, 22, 20, 16
C1, S1, W1, R1 = 26, 26, 24, 8
C2, S2, W2, R2 = 42, 40, 38, 36
DAMPING = 0.8
BASE_TAU = 16.0
VMEM = pl.BlockSpec(memory_space=pltpu.VMEM)
HBM = pl.BlockSpec(memory_space=pltpu.HBM)


def half_tau(level):
    return 0.5 * BASE_TAU / 4.0**level


def iota(shape, dim):
    return lax.broadcasted_iota(jnp.int32, shape, dim)


def dot(x, matrix):
    matrix = matrix.astype(jnp.bfloat16)
    total = None
    for _ in range(3):
        part = x.astype(jnp.bfloat16)
        x = x - part.astype(f32)
        term = jnp.dot(part, matrix, preferred_element_type=f32)
        total = term if total is None else total + term
    return total


def rounded(x):
    return x.astype(jnp.bfloat16).astype(f32)


def ahead(x, axis):
    return pltpu.roll(x, x.shape[axis] - 1, axis)


def behind(x, axis):
    return pltpu.roll(x, 1, axis)


def at(i, n):
    return pl.ds(i, n) if n > 1 or not isinstance(i, int) else slice(i, i + 1)


def by_rows(lo, hi, n, fn, carry=None):
    count = (hi - lo) // n
    if count > 1:
        carry = lax.fori_loop(0, count, lambda t, c: fn(lo + t * n, n, c), carry)
    elif count == 1:
        carry = fn(lo, n, carry)
    rest = hi - lo - count * n
    if rest:
        carry = fn(lo + count * n, rest, carry)
    return carry


def coefficients(level, m, cx, cy, cz, dg, wt, lo, hi, n, y_len, z_len):
    tau = half_tau(level)
    cx[lo - 1] = rounded(tau * (m[lo - 1] + m[lo]))

    def body(i, n, carry):
        here = m[at(i, n)]
        shape = here.shape
        lane = lax.rem(iota(shape, 2), z_len)
        z_last = lane == z_len - 1
        z_first = lane == 0
        edge = rounded(tau * here)
        x_up = rounded(tau * (here + m[at(i + 1, n)]))
        cx[at(i, n)] = x_up
        y_up = rounded(tau * (here + ahead(here, 1)))
        if y_len is None:
            y_down = behind(y_up, 1)
            cy[at(i, n)] = y_up
        else:
            sub = iota(shape, 1)
            inner = jnp.where(sub >= y_len - 1, 0.0, y_up)
            y_up = jnp.where(sub == y_len - 1, edge, y_up)
            y_down = jnp.where(sub == 0, edge, behind(inner, 1))
            cy[at(i, n)] = inner
        inner = jnp.where(z_last, 0.0, rounded(tau * (here + ahead(here, 2))))
        cz[at(i, n)] = inner
        z_up = jnp.where(z_last, edge, inner)
        z_down = jnp.where(z_first, edge, behind(inner, 2))
        diagonal = 1.0 + x_up + cx[at(i - 1, n)] + y_up + y_down + z_up + z_down
        if dg is not None:
            dg[at(i, n)] = diagonal
        wt[at(i, n)] = jnp.where(here > 0.0, DAMPING / diagonal, 0.0)
        return carry

    by_rows(lo, hi, n, body, 0)


def coupled(i, n, v, cx, cy, cz):
    here = v[at(i, n)]
    up = cy[at(i, n)]
    side = cz[at(i, n)]
    total = cx[at(i, n)] * v[at(i + 1, n)] + cx[at(i - 1, n)] * v[at(i - 1, n)]
    total = total + (up * ahead(here, 1) + behind(up * here, 1))
    return total + (side * ahead(here, 2) + behind(side * here, 2))


def residual(i, n, r, v, cx, cy, cz, dg):
    return r - dg[at(i, n)] * v[at(i, n)] + coupled(i, n, v, cx, cy, cz)


def relaxed(i, n, r, v, wt, cx, cy, cz, *_):
    return (1.0 - DAMPING) * v[at(i, n)] + wt[at(i, n)] * (r[at(i, n)] + coupled(i, n, v, cx, cy, cz))


def start(lo, hi, n, source, out, wt):
    def body(i, n, carry):
        for s, o in zip(source, out):
            o[at(i, n)] = wt[at(i, n)] * s[at(i, n)]
        return carry

    by_rows(lo, hi, n, body, 0)


def sweep(lo, hi, n, source, v, out, coefs, wt):
    def body(i, n, carry):
        for s, a, o in zip(source, v, out):
            o[at(i, n)] = relaxed(i, n, s, a, wt, *coefs)
        return carry

    by_rows(lo, hi, n, body, 0)


def pairs(x):
    x = x.reshape(x.shape[0] // 2, 2, *x.shape[1:])
    return x[:, 0] + x[:, 1]


def doubled(x):
    x = jnp.broadcast_to(x[:, None], (x.shape[0], 2, *x.shape[1:]))
    return x.reshape(x.shape[0] * 2, *x.shape[2:])


def flat_dot(x, matrix):
    n = x.shape[0] * x.shape[1]
    return dot(x.reshape(n, x.shape[2]), matrix).reshape(x.shape[0], x.shape[1], matrix.shape[1])


def fold_y(ref, k, n, first, count):
    return ref[k : k + n, pl.ds(first, count, stride=2), :] + ref[k : k + n, pl.ds(first + 1, count, stride=2), :]


def coarse_z(z_in, lanes_in, z_out, lanes_out, fields):
    src = iota((lanes_in, lanes_out), 0)
    dst = iota((lanes_in, lanes_out), 1)
    target = lax.div(src, z_in) * z_out + lax.div(lax.rem(src, z_in), 2)
    return jnp.where((target == dst) & (src < fields * z_in), 0.125, 0.0).astype(f32)


def fine_z(z_in, lanes_in, z_out, lanes_out, fields):
    src = iota((lanes_in, lanes_out), 0)
    dst = iota((lanes_in, lanes_out), 1)
    wanted = lax.div(dst, z_out) * z_in + lax.div(lax.rem(dst, z_out), 2)
    return jnp.where((wanted == src) & (dst < fields * z_out), 1.0, 0.0).astype(f32)


def products(i, n, s, c, us, uc, coefs, sums):
    num, den = sums
    v_s, v_c = us[at(i, n)], uc[at(i, n)]
    r_s, r_c = s[at(i, n)], c[at(i, n)]
    res_s = residual(i, n, r_s, us, *coefs)
    res_c = residual(i, n, r_c, uc, *coefs)
    num = num + jnp.sum(v_s * r_c + res_s * v_c, axis=0)
    den = den + jnp.sum(v_s * r_s + res_s * v_s, axis=0)
    return res_s, res_c, (num, den)


def fetch(sources, targets, sems):
    copies = [pltpu.make_async_copy(a, b, sems.at[k]) for k, (a, b) in enumerate(zip(sources, targets))]
    for copy in copies:
        copy.start()
    return copies


def wait(copies):
    for copy in copies:
        copy.wait()


def sides(low, high):
    even = lax.rem(lax.axis_index("wide"), 2) == 0
    return jnp.where(even, high, low), jnp.where(even, low, high)


def fetch0(own, inner, outer, fields, sems):
    sources, targets = [], []
    for index, ref in enumerate(fields):
        n = 3 if index else 4
        first = 4 + 3 * (index - 1) if index else 0
        inner_at, outer_at = sides(4 - n, 20)
        edges = ((inner, inner_at), (outer, outer_at))
        sources += [part.at[pl.ds(first, n)] for part, _ in edges]
        targets += [ref.at[pl.ds(lo, n)] for _, lo in edges]
        if own is not None:
            sources.append(own.at[index])
            targets.append(ref.at[pl.ds(4, 16)])
    return fetch(sources, targets, sems)


def fetch1(own, inner, outer, fields, sems):
    inner_at, outer_at = sides(2, 18)
    sources, targets = [], []
    for index, ref in fields:
        for source, lo in ((own, 10), (inner, inner_at), (outer, outer_at)):
            for j in range(4):
                sources.append(source.at[j, pl.ds(index * 8, 8)])
                targets.append(ref.at[pl.ds(lo, 8), pl.ds(8 * j, 8), :])
    return fetch(sources, targets, sems)


def down0(own, outer, inner, out, vs, vc, cx, cy, cz, dg, wt, ss, cc, m, us, uc, pair, thin, sems):
    copies = fetch0(None, inner, outer, (m, ss, cc), sems)
    for index, ref in enumerate((m, ss, cc)):
        ref[4:20] = own[index]
    wait(copies[:2])
    coefficients(0, m, cx, cy, cz, dg, wt, 1, 23, C0, None, 256)
    coefs = (cx, cy, cz, dg)
    wait(copies[2:])
    start(1, 23, S0, (ss, cc), (us, uc), wt)
    sweep(2, 22, W0, (ss, cc), (us, uc), (vs, vc), coefs, wt)

    def rest(i, n, sums):
        res_s, res_c, sums = products(i, n, ss, cc, vs, vc, coefs, sums)
        k = lax.div(i - 4, 2)
        pair[at(k, n // 2)] = pairs(res_s)
        pair[at(k + 8, n // 2)] = pairs(res_c)
        pair[at(k + 16, n // 2)] = pairs(m[at(i, n)])
        return sums

    zero = jnp.zeros((24, 256), f32)
    num, den = by_rows(4, 20, R0, rest, (zero, zero))
    thin[...] = flat_dot(pair[...], coarse_z(256, 256, 128, 128, 1))
    value = fold_y(thin, 0, 24, 4, 8)
    sub = iota((24, 256), 0)
    inside = (sub >= 4) & (sub < 20)
    num = jnp.sum(jnp.where(inside, num, 0.0))
    den = jnp.sum(jnp.where(inside, den, 0.0))
    lane = iota((8, 128), 1)
    both = jnp.where(lane == 0, num, jnp.where(lane == 1, den, 0.0))
    for j in range(4):
        out[j, 0:24] = value
        out[j, 24] = both


def down1(
    own, inner, outer, piece, mine,
    vs, vc, cx, cy, cz, dg, wt, ss, cc, m, us, uc, pair, thin, parts, sems,
):
    copies = fetch1(own, inner, outer, ((2, m), (0, ss), (1, cc)), sems)
    partial = fetch([own.at[j, 24] for j in range(4)], [parts.at[j] for j in range(4)], sems.at[pl.ds(36, 4)])
    wait(copies[:12])
    coefficients(1, m, cx, cy, cz, dg, wt, 3, 25, C1, 32, 128)
    coefs = (cx, cy, cz, dg)
    wait(copies[12:])
    wait(partial)
    start(3, 25, S1, (ss, cc), (us, uc), wt)
    sweep(4, 24, W1, (ss, cc), (us, uc), (vs, vc), coefs, wt)

    def rest(i, n, sums):
        res_s, res_c, sums = products(i, n, ss, cc, vs, vc, coefs, sums)
        k = (i - 6) // 2
        pair[at(k, n // 2), :, 0:128] = pairs(res_s)
        pair[at(k, n // 2), :, 128:256] = pairs(res_c)
        return sums

    zero = jnp.zeros((32, 128), f32)
    rest(6, 4, (zero, zero))
    num, den = rest(10, 8, (zero, zero))
    rest(18, 4, (zero, zero))
    both = pairs(m[2:26])
    pair[8:20, :, 0:128] = both
    pair[8:20, :, 128:256] = both
    thin[...] = flat_dot(pair[...], coarse_z(128, 256, 64, 128, 2))
    mid = fold_y(thin, 0, 8, 0, 16)
    mob = fold_y(thin, 8, 12, 0, 16)
    even = lax.rem(lax.axis_index("wide"), 2) == 0
    mine[0:8] = mid
    mine[8:20] = mob
    piece[0:8] = mid
    left = iota((4, 16, 128), 2) < 64
    piece[8:12] = jnp.where(
        left, jnp.where(even, mob[0:4], mob[4:8]), jnp.where(even, mob[4:8], mob[8:12])
    )
    lane = iota((8, 128), 1)
    num = jnp.sum(num) * 8.0
    den = jnp.sum(den) * 8.0
    finer = parts[0] + parts[1] + parts[2] + parts[3]
    total = finer + jnp.where(lane == 0, num, jnp.where(lane == 1, den, 0.0))
    for ref, row in ((piece, 12), (mine, 20)):
        ref[row] = jnp.concatenate([total, total], axis=0)


def bottom(
    mine, near, far, pair_own, pair_near, pair_far, e2_out, sums,
    m2, r2, u2, v2, cx2, cy2, cz2, dg2, wt2,
    m3, r3, u3, v3, cx3, cy3, cz3, dg3, wt3,
    m4, r4, u4, v4, cx4, cy4, cz4, dg4, wt4,
    pair2, thin2, pair3, thin3, wide3, wide2, e2, sems,
):
    left = iota((4, 16, 128), 2) < 64
    place = lax.axis_index("wide")
    size = lax.axis_size("wide")

    even = lax.rem(place, 2) == 0

    def choose(a, b):
        return jnp.where(even, a, b)

    def held(distance, value):
        return jnp.where((place + distance >= 0) & (place + distance < size), value, 0.0)

    def unpack(ref, distance):
        packed = held(distance, ref[8:12])
        other = pltpu.roll(packed, 64, 2)
        return held(distance, ref[0:8]), jnp.where(left, packed, other), jnp.where(left, other, packed)

    r2[18:26] = mine[0:8]
    m2[16:28] = mine[8:20]
    for ref, distance, r_at, m_at in (
        (near, choose(-2, 2), choose(10, 26), choose(8, 28)),
        (far, choose(-4, 4), choose(2, 34), choose(0, 36)),
        (pair_near, choose(3, -3), choose(30, 6), choose(32, 4)),
    ):
        cells, m_low, m_high = unpack(ref, distance)
        r2[pl.ds(r_at, 8)] = cells
        m2[pl.ds(m_at, 4)] = m_low
        m2[pl.ds(m_at + 4, 4)] = m_high
    cells, m_low, m_high = unpack(pair_own, 0)
    r2[pl.ds(choose(26, 14), 4)] = choose(cells[4:8], cells[0:4])
    m2[pl.ds(choose(28, 12), 4)] = choose(m_high, m_low)
    cells, m_low, m_high = unpack(pair_far, choose(5, -5))
    r2[pl.ds(choose(38, 2), 4)] = choose(cells[0:4], cells[4:8])
    m2[pl.ds(choose(40, 0), 4)] = choose(m_low, m_high)

    lo = jnp.where(even, jnp.where(place == 2, -2, 0), jnp.where(place == 3, -3, -2))
    hi = jnp.where(place == size - 4, 3, 2)

    def both_products(r, v, res, z_len, rows):
        num = v * pltpu.roll(r, 128 - z_len, 2)
        den = v * r
        if res is not None:
            num = num + res * pltpu.roll(v, 128 - z_len, 2)
            den = den + res * v
        device = lax.div(iota(v.shape, 0), rows) - 3
        mask = (iota(v.shape, 2) < z_len) & (device >= lo) & (device <= hi)
        num = jnp.sum(jnp.where(mask, num, 0.0), axis=0)
        den = jnp.sum(jnp.where(mask, den, 0.0), axis=0)
        return num, den

    c2 = (cx2, cy2, cz2, dg2)
    c3 = (cx3, cy3, cz3, dg3)
    c4 = (cx4, cy4, cz4, dg4)
    coefficients(2, m2, *c2, wt2, 1, 43, C2, 16, 64)
    start(2, 42, S2, (r2,), (u2,), wt2)
    sweep(3, 41, W2, (r2,), (u2,), (v2,), c2, wt2)

    res = residual(4, 36, r2[4:40], v2, *c2)
    pair2[0:18] = pairs(res)
    kept = slice(8, 36)
    num2, den2 = both_products(r2[kept], v2[kept], res[4:32], 64, 4)
    pair2[18:40] = pairs(m2[...])
    thin2[...] = flat_dot(pair2[...], coarse_z(64, 128, 32, 128, 2))
    r3[2:20] = fold_y(thin2, 0, 18, 0, 8)
    m3[...] = fold_y(thin2, 18, 22, 0, 8)

    coefficients(3, m3, *c3, wt3, 1, 21, 10, 8, 32)
    start(2, 20, 18, (r3,), (u3,), wt3)
    sweep(3, 19, 16, (r3,), (u3,), (v3,), c3, wt3)
    res = residual(4, 14, r3[4:18], v3, *c3)
    kept = slice(4, 18)
    num3, den3 = both_products(r3[kept], v3[kept], res, 32, 2)
    pair3[0:7] = pairs(res)
    pair3[7:18] = pairs(m3[...])
    thin3[...] = flat_dot(pair3[...], coarse_z(32, 128, 16, 128, 2))
    m4[...] = jnp.zeros((11, 8, 128), f32)
    r4[...] = jnp.zeros((11, 8, 128), f32)
    r4[2:9, 0:4, :] = fold_y(thin3, 0, 7, 0, 4)
    m4[:, 0:4, :] = fold_y(thin3, 7, 11, 0, 4)

    coefficients(4, m4, *c4, wt4, 1, 10, 9, 4, 16)
    u4[1] = jnp.zeros((8, 128), f32)
    u4[9] = jnp.zeros((8, 128), f32)
    start(2, 9, 7, (r4,), (u4,), wt4)
    sweep(2, 9, 7, (r4,), (u4,), (v4,), c4, wt4)
    wide3[:, pl.ds(0, 4, stride=2), :] = v4[3:8, 0:4, :]
    wide3[:, pl.ds(1, 4, stride=2), :] = v4[3:8, 0:4, :]
    v3[6:16] = v3[6:16] + doubled(flat_dot(wide3[...], fine_z(16, 128, 32, 128, 2)))
    sweep(7, 15, 8, (r3,), (v3,), (u3,), c3, wt3)
    sweep(8, 14, 6, (r3,), (u3,), (v3,), c3, wt3)
    wide2[:, pl.ds(0, 8, stride=2), :] = v3[8:14]
    wide2[:, pl.ds(1, 8, stride=2), :] = v3[8:14]
    v2[16:28] = v2[16:28] + doubled(flat_dot(wide2[...], fine_z(32, 128, 64, 128, 2)))
    sweep(17, 27, 10, (r2,), (v2,), (u2,), c2, wt2)
    e2[...] = relaxed(18, 8, r2, u2, wt2, *c2)
    copies = fetch([e2], [e2_out.at[pl.ds(0, 8)]], sems)
    kept = slice(2, 9)
    num4, den4 = both_products(r4[kept], v4[kept], None, 16, 1)
    num = 64.0 * jnp.sum(num2) + 512.0 * jnp.sum(num3) + 4096.0 * jnp.sum(num4)
    den = 64.0 * jnp.sum(den2) + 512.0 * jnp.sum(den3) + 4096.0 * jnp.sum(den4)
    lane = iota((8, 128), 1)
    finer = mine[20, 0:8] + near[12, 0:8] + pair_own[12, 0:8] + pair_near[12, 0:8]
    total = finer + jnp.where(lane == 0, num, jnp.where(lane == 1, den, 0.0))
    sums[...] = jnp.broadcast_to(total[0:1].reshape(1, 1, 128), sums.shape)
    wait(copies)


def up(
    e2_in, own1, inner1, outer1, own0, inner0, outer0, out_s, out_c,
    vs1, vc1, cx1, cy1, cz1, wt1, ss1, cc1, m1, as1, ac1, bs1, bc1,
    vs0, vc0, cx0, cy0, cz0, wt0, ss0, cc0, m0, as0, ac0, bs0, bc0,
    wide, add, block, thick, full, e2, sems,
):
    copies1 = fetch1(own1, inner1, outer1, ((2, m1), (0, ss1), (1, cc1)), sems)
    copies0 = fetch0(own0, inner0, outer0, (m0, ss0, cc0), sems.at[pl.ds(36, 9)])
    copies2 = fetch([e2_in.at[pl.ds(0, 8)]], [e2], sems.at[pl.ds(45, 1)])
    c1 = (cx1, cy1, cz1)
    c0 = (cx0, cy0, cz0)
    wait(copies1)
    coefficients(1, m1, cx1, cy1, cz1, None, wt1, 5, 23, C1, 32, 128)
    start(5, 23, S1, (ss1, cc1), (as1, ac1), wt1)
    sweep(6, 22, W1, (ss1, cc1), (as1, ac1), (vs1, vc1), c1, wt1)
    wait(copies0)
    coefficients(0, m0, cx0, cy0, cz0, None, wt0, 1, 23, C0, None, 256)
    start(1, 23, S0, (ss0, cc0), (as0, ac0), wt0)
    sweep(2, 22, W0, (ss0, cc0), (as0, ac0), (vs0, vc0), c0, wt0)
    wait(copies2)
    wide[:, pl.ds(0, 16, stride=2), :] = e2[...]
    wide[:, pl.ds(1, 16, stride=2), :] = e2[...]
    add[...] = flat_dot(wide[...], fine_z(64, 128, 128, 256, 2))

    def correct1(i, n, carry):
        k = lax.div(i - 6, 2)
        both = add[at(k, n // 2)]
        as1[at(i, n)] = vs1[at(i, n)] + doubled(both[:, :, 0:128])
        ac1[at(i, n)] = vc1[at(i, n)] + doubled(both[:, :, 128:256])
        return carry

    by_rows(6, 22, R1, correct1, 0)
    sweep(8, 20, W1, (ss1, cc1), (as1, ac1), (bs1, bc1), c1, wt1)
    place = lax.axis_index("narrow")
    block[:, 0:8, :] = jnp.zeros((20, 8, 128), f32)
    block[:, 40:48, :] = jnp.zeros((20, 8, 128), f32)

    def last1(i, n, carry):
        for index, (r, v) in enumerate(((ss1, bs1), (cc1, bc1))):
            value = relaxed(i, n, r, v, wt1, *c1)
            block[at(index * 10 + i - 9, n), 8:40, :] = value
        return carry

    by_rows(9, 19, 5, last1, 0)
    value = block[:, pl.ds(pl.multiple_of(8 * place, 8), 24), :][:, 6:18, :]
    thick[:, pl.ds(0, 12, stride=2), :] = value
    thick[:, pl.ds(1, 12, stride=2), :] = value
    full[...] = flat_dot(thick[...], fine_z(128, 128, 256, 256, 1))

    def correct0(i, n, carry):
        k = lax.div(i - 2, 2)
        as0[at(i, n)] = vs0[at(i, n)] + doubled(full[at(k, n // 2)])
        ac0[at(i, n)] = vc0[at(i, n)] + doubled(full[at(10 + k, n // 2)])
        return carry

    by_rows(2, 22, R0, correct0, 0)
    sweep(3, 21, W0, (ss0, cc0), (as0, ac0), (bs0, bc0), c0, wt0)

    def last0(i, n, carry):
        for r, v, o in ((ss0, bs0, out_s), (cc0, bc0, out_c)):
            o[at(i - 4, n)] = relaxed(i, n, r, v, wt0, *c0)[:, 4:20, :]
        return carry

    by_rows(4, 20, W0, last0, 0)


def final(every, out_s, out_c, out, held, sems):
    total = jnp.sum(every[...], axis=0)
    lane = iota((1, 128), 1)
    num = jnp.sum(jnp.where(lane == 0, total, 0.0), axis=1, keepdims=True)
    den = jnp.sum(jnp.where(lane == 1, total, 0.0), axis=1, keepdims=True)
    ratio = (num / (1.0 + den))[0, 0]
    copies = []
    for k in range(4):
        rows = pl.ds(4 * k, 4)
        held[rows] = out_c[rows] - ratio * out_s[rows]
        copies += fetch([held.at[rows]], [out.at[rows]], sems.at[pl.ds(k, 1)])
    wait(copies)


def call(kernel, ins, outs, scratch, name, sems=0, specs=None, out_specs=None):
    scratch = [pltpu.VMEM(s, f32) for s in scratch]
    if sems:
        scratch.append(pltpu.SemaphoreType.DMA((sems,)))
    return pl.pallas_call(
        kernel,
        out_shape=[jax.ShapeDtypeStruct(s, f32) for s in outs],
        in_specs=specs or [VMEM] * len(ins),
        out_specs=out_specs or [VMEM] * len(outs),
        scratch_shapes=scratch,
        compiler_params=pltpu.CompilerParams(vmem_limit_bytes=LIMIT * 2**20),
        name=name,
    )(*ins)


def shifted(value, axis, by):
    size = lax.axis_size(axis)
    return lax.ppermute(value, axis, [(i, i + by) for i in range(size) if 0 <= i + by < size])


def apart(value, by):
    size = lax.axis_size("wide")
    return lax.ppermute(value, "wide", [(i, (i + by * (1 - 2 * (i % 2))) % size) for i in range(size)])


def swapped(value, first):
    pairs = [(i, i + 1) for i in range(first, lax.axis_size("wide") - 1, 2)]
    return lax.ppermute(value, "wide", pairs + [(b, a) for a, b in pairs])


def per_device(mobility, sav_vector, cotangent):
    whole = jnp.stack([mobility, sav_vector, cotangent])
    y_lo = shifted(whole[:, :, -HALO:], "narrow", 1)
    y_hi = shifted(whole[:, :, :HALO], "narrow", -1)
    own = jnp.concatenate([y_lo, whole, y_hi], axis=2)
    odd = lax.rem(lax.axis_index("wide"), 2)

    def edge(at_end):
        return jnp.concatenate(
            [
                lax.dynamic_slice_in_dim(own[index], at_end * (16 - n), n, axis=0)
                for index, n in enumerate((HALO, HALO - 1, HALO - 1))
            ]
        )

    x_inner = swapped(edge(1 - odd), 0)
    x_outer = swapped(edge(odd), 1)
    a0 = (24, 24, 256)
    (chunk,) = call(
        down0,
        (own, x_outer, x_inner),
        [(4, 25, 8, 128)],
        [a0] * 13 + [(24, 24, 128)],
        "down0",
        6,
        [VMEM] + [HBM] * 2,
    )
    gathered = lax.all_to_all(chunk, "narrow", 0, 0)
    outer = swapped(gathered, 1)
    inner = swapped(gathered, 0)
    a1 = (28, 32, 128)
    piece, mine = call(
        down1,
        (gathered, inner, outer),
        [(13, 16, 128), (21, 16, 128)],
        [a1] * 12 + [(20, 32, 256), (20, 32, 128), (4, 8, 128)],
        "down1",
        40,
        [HBM] * 3,
    )
    near = apart(piece, 2)
    far = apart(piece, 4)
    pair_own = swapped(piece, 0)
    pair_near = swapped(near, 0)
    pair_far = swapped(far, 0)
    wide = lax.axis_size("wide")
    e2, sums = call(
        bottom,
        (mine, near, far, pair_own, pair_near, pair_far),
        [(ROOM, 16, 128), (wide // 4, 1, 128)],
        [(44, 16, 128)] * 9
        + [(22, 8, 128)] * 9
        + [(11, 8, 128)] * 9
        + [(40, 16, 128)] * 2
        + [(18, 8, 128)] * 2
        + [(5, 8, 128), (6, 16, 128), (8, 16, 128)],
        "bottom",
        1,
        None,
        [HBM, VMEM],
    )
    groups = [[i for i in range(wide) if (i // 2 + 2 * (i % 2)) % 4 == s] for s in range(4)]
    y_lo, y_hi, mobility, sav_vector, cotangent, sums = lax.optimization_barrier(
        (y_lo, y_hi, mobility, sav_vector, cotangent, sums)
    )
    every = lax.all_to_all(sums, "wide", 0, 0, axis_index_groups=groups)
    again = jnp.concatenate([y_lo, jnp.stack([mobility, sav_vector, cotangent]), y_hi], axis=2)
    out_s, out_c = call(
        up,
        (e2, gathered, inner, outer, again, x_inner, x_outer),
        [(16, 16, 256)] * 2,
        [a1] * 13
        + [a0] * 13
        + [(8, 32, 128), (8, 32, 256), (20, 48, 128), (20, 24, 128), (20, 24, 256), (8, 16, 128)],
        "up",
        46,
        [HBM] * 7,
    )
    return call(final, (every, out_s, out_c), [(16, 16, 256)], [(16, 16, 256)], "final", 4, None, [HBM])[0]


def solution(mesh):
    spec = P("wide", "narrow", None)
    return jax.shard_map(
        per_device, mesh=mesh, in_specs=(spec, spec, spec), out_specs=spec, check_vma=False
    )
```

```python
import functools

import jax
import jax.numpy as jnp
from jax import lax
from jax.experimental import pallas as pl
from jax.experimental.pallas import tpu as pltpu
from jax.sharding import PartitionSpec as P

f32 = jnp.float32
HALO = 4
LIMIT = 24
ROOM = 6144
C0, S0, W0, R0 = 22, 22, 20, 16
C1, S1, W1, R1 = 26, 26, 24, 8
C2, S2, W2, R2 = 42, 40, 38, 36
DAMPING = 0.8
BASE_TAU = 16.0
VMEM = pl.BlockSpec(memory_space=pltpu.VMEM)
HBM = pl.BlockSpec(memory_space=pltpu.HBM)


def half_tau(level):
    return 0.5 * BASE_TAU / 4.0**level


def iota(shape, dim):
    return lax.broadcasted_iota(jnp.int32, shape, dim)


def dot(x, matrix):
    matrix = matrix.astype(jnp.bfloat16)
    total = None
    for _ in range(3):
        part = x.astype(jnp.bfloat16)
        x = x - part.astype(f32)
        term = jnp.dot(part, matrix, preferred_element_type=f32)
        total = term if total is None else total + term
    return total


def rounded(x):
    return x.astype(jnp.bfloat16).astype(f32)


def ahead(x, axis):
    return pltpu.roll(x, x.shape[axis] - 1, axis)


def behind(x, axis):
    return pltpu.roll(x, 1, axis)


def at(i, n):
    return pl.ds(i, n) if n > 1 or not isinstance(i, int) else slice(i, i + 1)


def by_rows(lo, hi, n, fn, carry=None):
    count = (hi - lo) // n
    if count > 1:
        carry = lax.fori_loop(0, count, lambda t, c: fn(lo + t * n, n, c), carry)
    elif count == 1:
        carry = fn(lo, n, carry)
    rest = hi - lo - count * n
    if rest:
        carry = fn(lo + count * n, rest, carry)
    return carry


def coefficients(level, m, cx, cy, cz, dg, wt, lo, hi, n, y_len, z_len):
    tau = half_tau(level)
    cx[lo - 1] = rounded(tau * (m[lo - 1] + m[lo]))

    def body(i, n, carry):
        here = m[at(i, n)]
        shape = here.shape
        lane = lax.rem(iota(shape, 2), z_len)
        z_last = lane == z_len - 1
        z_first = lane == 0
        edge = rounded(tau * here)
        x_up = rounded(tau * (here + m[at(i + 1, n)]))
        cx[at(i, n)] = x_up
        y_up = rounded(tau * (here + ahead(here, 1)))
        if y_len is None:
            y_down = behind(y_up, 1)
            cy[at(i, n)] = y_up
        else:
            sub = iota(shape, 1)
            inner = jnp.where(sub >= y_len - 1, 0.0, y_up)
            y_up = jnp.where(sub == y_len - 1, edge, y_up)
            y_down = jnp.where(sub == 0, edge, behind(inner, 1))
            cy[at(i, n)] = inner
        inner = jnp.where(z_last, 0.0, rounded(tau * (here + ahead(here, 2))))
        cz[at(i, n)] = inner
        z_up = jnp.where(z_last, edge, inner)
        z_down = jnp.where(z_first, edge, behind(inner, 2))
        diagonal = 1.0 + x_up + cx[at(i - 1, n)] + y_up + y_down + z_up + z_down
        if dg is not None:
            dg[at(i, n)] = diagonal
        wt[at(i, n)] = jnp.where(here > 0.0, DAMPING / diagonal, 0.0)
        return carry

    by_rows(lo, hi, n, body, 0)


def coupled(i, n, v, cx, cy, cz):
    here = v[at(i, n)]
    up = cy[at(i, n)]
    side = cz[at(i, n)]
    total = cx[at(i, n)] * v[at(i + 1, n)] + cx[at(i - 1, n)] * v[at(i - 1, n)]
    total = total + (up * ahead(here, 1) + behind(up * here, 1))
    return total + (side * ahead(here, 2) + behind(side * here, 2))


def residual(i, n, r, v, cx, cy, cz, dg):
    return r - dg[at(i, n)] * v[at(i, n)] + coupled(i, n, v, cx, cy, cz)


def relaxed(i, n, r, v, wt, cx, cy, cz, *_):
    return (1.0 - DAMPING) * v[at(i, n)] + wt[at(i, n)] * (r[at(i, n)] + coupled(i, n, v, cx, cy, cz))


def start(lo, hi, n, source, out, wt):
    def body(i, n, carry):
        for s, o in zip(source, out):
            o[at(i, n)] = wt[at(i, n)] * s[at(i, n)]
        return carry

    by_rows(lo, hi, n, body, 0)


def sweep(lo, hi, n, source, v, out, coefs, wt):
    def body(i, n, carry):
        for s, a, o in zip(source, v, out):
            o[at(i, n)] = relaxed(i, n, s, a, wt, *coefs)
        return carry

    by_rows(lo, hi, n, body, 0)


def pairs(x):
    x = x.reshape(x.shape[0] // 2, 2, *x.shape[1:])
    return x[:, 0] + x[:, 1]


def doubled(x):
    x = jnp.broadcast_to(x[:, None], (x.shape[0], 2, *x.shape[1:]))
    return x.reshape(x.shape[0] * 2, *x.shape[2:])


def flat_dot(x, matrix):
    n = x.shape[0] * x.shape[1]
    return dot(x.reshape(n, x.shape[2]), matrix).reshape(x.shape[0], x.shape[1], matrix.shape[1])


def fold_y(ref, k, n, first, count):
    return ref[k : k + n, pl.ds(first, count, stride=2), :] + ref[k : k + n, pl.ds(first + 1, count, stride=2), :]


def coarse_z(z_in, lanes_in, z_out, lanes_out, fields):
    src = iota((lanes_in, lanes_out), 0)
    dst = iota((lanes_in, lanes_out), 1)
    target = lax.div(src, z_in) * z_out + lax.div(lax.rem(src, z_in), 2)
    return jnp.where((target == dst) & (src < fields * z_in), 0.125, 0.0).astype(f32)


def fine_z(z_in, lanes_in, z_out, lanes_out, fields):
    src = iota((lanes_in, lanes_out), 0)
    dst = iota((lanes_in, lanes_out), 1)
    wanted = lax.div(dst, z_out) * z_in + lax.div(lax.rem(dst, z_out), 2)
    return jnp.where((wanted == src) & (dst < fields * z_out), 1.0, 0.0).astype(f32)


def products(i, n, s, c, us, uc, coefs, sums):
    num, den = sums
    v_s, v_c = us[at(i, n)], uc[at(i, n)]
    r_s, r_c = s[at(i, n)], c[at(i, n)]
    res_s = residual(i, n, r_s, us, *coefs)
    res_c = residual(i, n, r_c, uc, *coefs)
    num = num + jnp.sum(v_s * r_c + res_s * v_c, axis=0)
    den = den + jnp.sum(v_s * r_s + res_s * v_s, axis=0)
    return res_s, res_c, (num, den)


def fetch(sources, targets, sems):
    copies = [pltpu.make_async_copy(a, b, sems.at[k]) for k, (a, b) in enumerate(zip(sources, targets))]
    for copy in copies:
        copy.start()
    return copies


def wait(copies):
    for copy in copies:
        copy.wait()


def sides(low, high):
    even = lax.rem(lax.axis_index("wide"), 2) == 0
    return jnp.where(even, high, low), jnp.where(even, low, high)


def fetch0(own, inner, outer, fields, sems):
    sources, targets = [], []
    for index, ref in enumerate(fields):
        n = 3 if index else 4
        first = 4 + 3 * (index - 1) if index else 0
        inner_at, outer_at = sides(4 - n, 20)
        edges = ((inner, inner_at), (outer, outer_at))
        sources += [part.at[pl.ds(first, n)] for part, _ in edges]
        targets += [ref.at[pl.ds(lo, n)] for _, lo in edges]
        if own is not None:
            sources.append(own.at[index])
            targets.append(ref.at[pl.ds(4, 16)])
    return fetch(sources, targets, sems)


def fetch1(own, inner, outer, fields, sems):
    inner_at, outer_at = sides(2, 18)
    sources, targets = [], []
    for index, ref in fields:
        for source, lo in ((own, 10), (inner, inner_at), (outer, outer_at)):
            for j in range(4):
                sources.append(source.at[j, pl.ds(index * 8, 8)])
                targets.append(ref.at[pl.ds(lo, 8), pl.ds(8 * j, 8), :])
    return fetch(sources, targets, sems)


def down0(own, outer, inner, out, vs, vc, cx, cy, cz, dg, wt, ss, cc, m, us, uc, pair, thin, sems):
    copies = fetch0(None, inner, outer, (m, ss, cc), sems)
    for index, ref in enumerate((m, ss, cc)):
        ref[4:20] = own[index]
    wait(copies[:2])
    coefficients(0, m, cx, cy, cz, dg, wt, 1, 23, C0, None, 256)
    coefs = (cx, cy, cz, dg)
    wait(copies[2:])
    start(1, 23, S0, (ss, cc), (us, uc), wt)
    sweep(2, 22, W0, (ss, cc), (us, uc), (vs, vc), coefs, wt)

    def rest(i, n, sums):
        res_s, res_c, sums = products(i, n, ss, cc, vs, vc, coefs, sums)
        k = lax.div(i - 4, 2)
        pair[at(k, n // 2)] = pairs(res_s)
        pair[at(k + 8, n // 2)] = pairs(res_c)
        pair[at(k + 16, n // 2)] = pairs(m[at(i, n)])
        return sums

    zero = jnp.zeros((24, 256), f32)
    num, den = by_rows(4, 20, R0, rest, (zero, zero))
    thin[...] = flat_dot(pair[...], coarse_z(256, 256, 128, 128, 1))
    value = fold_y(thin, 0, 24, 4, 8)
    sub = iota((24, 256), 0)
    inside = (sub >= 4) & (sub < 20)
    num = jnp.sum(jnp.where(inside, num, 0.0))
    den = jnp.sum(jnp.where(inside, den, 0.0))
    lane = iota((8, 128), 1)
    both = jnp.where(lane == 0, num, jnp.where(lane == 1, den, 0.0))
    for j in range(4):
        out[j, 0:24] = value
        out[j, 24] = both


def down1(
    own, inner, outer, piece, mine,
    vs, vc, cx, cy, cz, dg, wt, ss, cc, m, us, uc, pair, thin, parts, sems,
):
    copies = fetch1(own, inner, outer, ((2, m), (0, ss), (1, cc)), sems)
    partial = fetch([own.at[j, 24] for j in range(4)], [parts.at[j] for j in range(4)], sems.at[pl.ds(36, 4)])
    wait(copies[:12])
    coefficients(1, m, cx, cy, cz, dg, wt, 3, 25, C1, 32, 128)
    coefs = (cx, cy, cz, dg)
    wait(copies[12:])
    wait(partial)
    start(3, 25, S1, (ss, cc), (us, uc), wt)
    sweep(4, 24, W1, (ss, cc), (us, uc), (vs, vc), coefs, wt)

    def rest(i, n, sums):
        res_s, res_c, sums = products(i, n, ss, cc, vs, vc, coefs, sums)
        k = (i - 6) // 2
        pair[at(k, n // 2), :, 0:128] = pairs(res_s)
        pair[at(k, n // 2), :, 128:256] = pairs(res_c)
        return sums

    zero = jnp.zeros((32, 128), f32)
    rest(6, 4, (zero, zero))
    num, den = rest(10, 8, (zero, zero))
    rest(18, 4, (zero, zero))
    both = pairs(m[2:26])
    pair[8:20, :, 0:128] = both
    pair[8:20, :, 128:256] = both
    thin[...] = flat_dot(pair[...], coarse_z(128, 256, 64, 128, 2))
    mid = fold_y(thin, 0, 8, 0, 16)
    mob = fold_y(thin, 8, 12, 0, 16)
    even = lax.rem(lax.axis_index("wide"), 2) == 0
    mine[0:8] = mid
    mine[8:20] = mob
    piece[0:8] = mid
    left = iota((4, 16, 128), 2) < 64
    piece[8:12] = jnp.where(
        left, jnp.where(even, mob[0:4], mob[4:8]), jnp.where(even, mob[4:8], mob[8:12])
    )
    lane = iota((8, 128), 1)
    num = jnp.sum(num) * 8.0
    den = jnp.sum(den) * 8.0
    finer = parts[0] + parts[1] + parts[2] + parts[3]
    total = finer + jnp.where(lane == 0, num, jnp.where(lane == 1, den, 0.0))
    for ref, row in ((piece, 12), (mine, 20)):
        ref[row] = jnp.concatenate([total, total], axis=0)


def bottom(
    mine, far, near, pair_own, pair_far, pair_near, e2_out, sums,
    m2, r2, u2, v2, cx2, cy2, cz2, dg2, wt2,
    m3, r3, u3, v3, cx3, cy3, cz3, dg3, wt3,
    m4, r4, u4, v4, cx4, cy4, cz4, dg4, wt4,
    pair2, thin2, pair3, thin3, wide3, wide2, e2, sems,
):
    left = iota((4, 16, 128), 2) < 64
    place = lax.axis_index("wide")
    size = lax.axis_size("wide")

    even = lax.rem(place, 2) == 0

    def choose(a, b):
        return jnp.where(even, a, b)

    def held(distance, value):
        return jnp.where((place + distance >= 0) & (place + distance < size), value, 0.0)

    def unpack(ref, distance):
        packed = held(distance, ref[8:12])
        other = pltpu.roll(packed, 64, 2)
        return held(distance, ref[0:8]), jnp.where(left, packed, other), jnp.where(left, other, packed)

    r2[18:26] = mine[0:8]
    m2[16:28] = mine[8:20]
    for ref, distance, r_at, m_at in (
        (near, choose(-2, 2), choose(10, 26), choose(8, 28)),
        (far, choose(-4, 4), choose(2, 34), choose(0, 36)),
        (pair_near, choose(3, -3), choose(30, 6), choose(32, 4)),
    ):
        cells, m_low, m_high = unpack(ref, distance)
        r2[pl.ds(r_at, 8)] = cells
        m2[pl.ds(m_at, 4)] = m_low
        m2[pl.ds(m_at + 4, 4)] = m_high
    cells, m_low, m_high = unpack(pair_own, 0)
    r2[pl.ds(choose(26, 14), 4)] = choose(cells[4:8], cells[0:4])
    m2[pl.ds(choose(28, 12), 4)] = choose(m_high, m_low)
    cells, m_low, m_high = unpack(pair_far, choose(5, -5))
    r2[pl.ds(choose(38, 2), 4)] = choose(cells[0:4], cells[4:8])
    m2[pl.ds(choose(40, 0), 4)] = choose(m_low, m_high)

    lo = jnp.where(even, jnp.where(place == 2, -2, 0), jnp.where(place == 3, -3, -2))
    hi = jnp.where(place == size - 4, 3, 2)

    def both_products(r, v, res, z_len, rows):
        num = v * pltpu.roll(r, 128 - z_len, 2)
        den = v * r
        if res is not None:
            num = num + res * pltpu.roll(v, 128 - z_len, 2)
            den = den + res * v
        device = lax.div(iota(v.shape, 0), rows) - 3
        mask = (iota(v.shape, 2) < z_len) & (device >= lo) & (device <= hi)
        num = jnp.sum(jnp.where(mask, num, 0.0), axis=0)
        den = jnp.sum(jnp.where(mask, den, 0.0), axis=0)
        return num, den

    c2 = (cx2, cy2, cz2, dg2)
    c3 = (cx3, cy3, cz3, dg3)
    c4 = (cx4, cy4, cz4, dg4)
    coefficients(2, m2, *c2, wt2, 1, 43, C2, 16, 64)
    start(2, 42, S2, (r2,), (u2,), wt2)
    sweep(3, 41, W2, (r2,), (u2,), (v2,), c2, wt2)

    res = residual(4, 36, r2[4:40], v2, *c2)
    pair2[0:18] = pairs(res)
    kept = slice(8, 36)
    num2, den2 = both_products(r2[kept], v2[kept], res[4:32], 64, 4)
    pair2[18:40] = pairs(m2[...])
    thin2[...] = flat_dot(pair2[...], coarse_z(64, 128, 32, 128, 2))
    r3[2:20] = fold_y(thin2, 0, 18, 0, 8)
    m3[...] = fold_y(thin2, 18, 22, 0, 8)

    coefficients(3, m3, *c3, wt3, 1, 21, 10, 8, 32)
    start(2, 20, 18, (r3,), (u3,), wt3)
    sweep(3, 19, 16, (r3,), (u3,), (v3,), c3, wt3)
    res = residual(4, 14, r3[4:18], v3, *c3)
    kept = slice(4, 18)
    num3, den3 = both_products(r3[kept], v3[kept], res, 32, 2)
    pair3[0:7] = pairs(res)
    pair3[7:18] = pairs(m3[...])
    thin3[...] = flat_dot(pair3[...], coarse_z(32, 128, 16, 128, 2))
    m4[...] = jnp.zeros((11, 8, 128), f32)
    r4[...] = jnp.zeros((11, 8, 128), f32)
    r4[2:9, 0:4, :] = fold_y(thin3, 0, 7, 0, 4)
    m4[:, 0:4, :] = fold_y(thin3, 7, 11, 0, 4)

    coefficients(4, m4, *c4, wt4, 1, 10, 9, 4, 16)
    u4[1] = jnp.zeros((8, 128), f32)
    u4[9] = jnp.zeros((8, 128), f32)
    start(2, 9, 7, (r4,), (u4,), wt4)
    sweep(2, 9, 7, (r4,), (u4,), (v4,), c4, wt4)
    wide3[:, pl.ds(0, 4, stride=2), :] = v4[3:8, 0:4, :]
    wide3[:, pl.ds(1, 4, stride=2), :] = v4[3:8, 0:4, :]
    v3[6:16] = v3[6:16] + doubled(flat_dot(wide3[...], fine_z(16, 128, 32, 128, 2)))
    sweep(7, 15, 8, (r3,), (v3,), (u3,), c3, wt3)
    sweep(8, 14, 6, (r3,), (u3,), (v3,), c3, wt3)
    wide2[:, pl.ds(0, 8, stride=2), :] = v3[8:14]
    wide2[:, pl.ds(1, 8, stride=2), :] = v3[8:14]
    v2[16:28] = v2[16:28] + doubled(flat_dot(wide2[...], fine_z(32, 128, 64, 128, 2)))
    sweep(17, 27, 10, (r2,), (v2,), (u2,), c2, wt2)
    e2[...] = relaxed(18, 8, r2, u2, wt2, *c2)
    copies = fetch([e2], [e2_out.at[pl.ds(0, 8)]], sems)
    kept = slice(2, 9)
    num4, den4 = both_products(r4[kept], v4[kept], None, 16, 1)
    num = 64.0 * jnp.sum(num2) + 512.0 * jnp.sum(num3) + 4096.0 * jnp.sum(num4)
    den = 64.0 * jnp.sum(den2) + 512.0 * jnp.sum(den3) + 4096.0 * jnp.sum(den4)
    lane = iota((8, 128), 1)
    finer = mine[20, 0:8] + near[12, 0:8] + pair_own[12, 0:8] + pair_near[12, 0:8]
    total = finer + jnp.where(lane == 0, num, jnp.where(lane == 1, den, 0.0))
    sums[...] = jnp.broadcast_to(total[0:1].reshape(1, 1, 128), sums.shape)
    wait(copies)


def up(
    e2_in, own1, inner1, outer1, own0, inner0, outer0, out_s, out_c,
    vs1, vc1, cx1, cy1, cz1, wt1, ss1, cc1, m1, as1, ac1, bs1, bc1,
    vs0, vc0, cx0, cy0, cz0, wt0, ss0, cc0, m0, as0, ac0, bs0, bc0,
    wide, add, block, thick, full, e2, sems,
):
    copies1 = fetch1(own1, inner1, outer1, ((2, m1), (0, ss1), (1, cc1)), sems)
    copies0 = fetch0(own0, inner0, outer0, (m0, ss0, cc0), sems.at[pl.ds(36, 9)])
    copies2 = fetch([e2_in.at[pl.ds(0, 8)]], [e2], sems.at[pl.ds(45, 1)])
    c1 = (cx1, cy1, cz1)
    c0 = (cx0, cy0, cz0)
    wait(copies1)
    coefficients(1, m1, cx1, cy1, cz1, None, wt1, 5, 23, C1, 32, 128)
    start(5, 23, S1, (ss1, cc1), (as1, ac1), wt1)
    sweep(6, 22, W1, (ss1, cc1), (as1, ac1), (vs1, vc1), c1, wt1)
    wait(copies0)
    coefficients(0, m0, cx0, cy0, cz0, None, wt0, 1, 23, C0, None, 256)
    start(1, 23, S0, (ss0, cc0), (as0, ac0), wt0)
    sweep(2, 22, W0, (ss0, cc0), (as0, ac0), (vs0, vc0), c0, wt0)
    wait(copies2)
    wide[:, pl.ds(0, 16, stride=2), :] = e2[...]
    wide[:, pl.ds(1, 16, stride=2), :] = e2[...]
    add[...] = flat_dot(wide[...], fine_z(64, 128, 128, 256, 2))

    def correct1(i, n, carry):
        k = lax.div(i - 6, 2)
        both = add[at(k, n // 2)]
        as1[at(i, n)] = vs1[at(i, n)] + doubled(both[:, :, 0:128])
        ac1[at(i, n)] = vc1[at(i, n)] + doubled(both[:, :, 128:256])
        return carry

    by_rows(6, 22, R1, correct1, 0)
    sweep(8, 20, W1, (ss1, cc1), (as1, ac1), (bs1, bc1), c1, wt1)
    place = lax.axis_index("narrow")
    block[:, 0:8, :] = jnp.zeros((20, 8, 128), f32)
    block[:, 40:48, :] = jnp.zeros((20, 8, 128), f32)

    def last1(i, n, carry):
        for index, (r, v) in enumerate(((ss1, bs1), (cc1, bc1))):
            value = relaxed(i, n, r, v, wt1, *c1)
            block[at(index * 10 + i - 9, n), 8:40, :] = value
        return carry

    by_rows(9, 19, 5, last1, 0)
    value = block[:, pl.ds(pl.multiple_of(8 * place, 8), 24), :][:, 6:18, :]
    thick[:, pl.ds(0, 12, stride=2), :] = value
    thick[:, pl.ds(1, 12, stride=2), :] = value
    full[...] = flat_dot(thick[...], fine_z(128, 128, 256, 256, 1))

    def correct0(i, n, carry):
        k = lax.div(i - 2, 2)
        as0[at(i, n)] = vs0[at(i, n)] + doubled(full[at(k, n // 2)])
        ac0[at(i, n)] = vc0[at(i, n)] + doubled(full[at(10 + k, n // 2)])
        return carry

    by_rows(2, 22, R0, correct0, 0)
    sweep(3, 21, W0, (ss0, cc0), (as0, ac0), (bs0, bc0), c0, wt0)

    def last0(i, n, carry):
        for r, v, o in ((ss0, bs0, out_s), (cc0, bc0, out_c)):
            o[at(i - 4, n)] = relaxed(i, n, r, v, wt0, *c0)[:, 4:20, :]
        return carry

    by_rows(4, 20, W0, last0, 0)


def final(every, out_s, out_c, out, held, sems):
    total = jnp.sum(every[...], axis=0)
    lane = iota((1, 128), 1)
    num = jnp.sum(jnp.where(lane == 0, total, 0.0), axis=1, keepdims=True)
    den = jnp.sum(jnp.where(lane == 1, total, 0.0), axis=1, keepdims=True)
    ratio = (num / (1.0 + den))[0, 0]
    copies = []
    for k in range(4):
        rows = pl.ds(4 * k, 4)
        held[rows] = out_c[rows] - ratio * out_s[rows]
        copies += fetch([held.at[rows]], [out.at[rows]], sems.at[pl.ds(k, 1)])
    wait(copies)


def call(kernel, ins, outs, scratch, name, sems=0, specs=None, out_specs=None):
    scratch = [pltpu.VMEM(s, f32) for s in scratch]
    if sems:
        scratch.append(pltpu.SemaphoreType.DMA((sems,)))
    return pl.pallas_call(
        kernel,
        out_shape=[jax.ShapeDtypeStruct(s, f32) for s in outs],
        in_specs=specs or [VMEM] * len(ins),
        out_specs=out_specs or [VMEM] * len(outs),
        scratch_shapes=scratch,
        compiler_params=pltpu.CompilerParams(vmem_limit_bytes=LIMIT * 2**20),
        name=name,
    )(*ins)


def shifted(value, axis, by):
    size = lax.axis_size(axis)
    return lax.ppermute(value, axis, [(i, i + by) for i in range(size) if 0 <= i + by < size])


def apart(value, by):
    size = lax.axis_size("wide")
    return lax.ppermute(value, "wide", [(i, (i + by * (1 - 2 * (i % 2))) % size) for i in range(size)])


def swapped(value, first):
    pairs = [(i, i + 1) for i in range(first, lax.axis_size("wide") - 1, 2)]
    return lax.ppermute(value, "wide", pairs + [(b, a) for a, b in pairs])


def per_device(mobility, sav_vector, cotangent):
    whole = jnp.stack([mobility, sav_vector, cotangent])
    y_lo = shifted(whole[:, :, -HALO:], "narrow", 1)
    y_hi = shifted(whole[:, :, :HALO], "narrow", -1)
    own = jnp.concatenate([y_lo, whole, y_hi], axis=2)
    odd = lax.rem(lax.axis_index("wide"), 2)

    def edge(at_end):
        return jnp.concatenate(
            [
                lax.dynamic_slice_in_dim(own[index], at_end * (16 - n), n, axis=0)
                for index, n in enumerate((HALO, HALO - 1, HALO - 1))
            ]
        )

    x_inner = swapped(edge(1 - odd), 0)
    x_outer = swapped(edge(odd), 1)
    a0 = (24, 24, 256)
    (chunk,) = call(
        down0,
        (own, x_outer, x_inner),
        [(4, 25, 8, 128)],
        [a0] * 13 + [(24, 24, 128)],
        "down0",
        6,
        [VMEM] + [HBM] * 2,
    )
    gathered = lax.all_to_all(chunk, "narrow", 0, 0)
    outer = swapped(gathered, 1)
    inner = swapped(gathered, 0)
    a1 = (28, 32, 128)
    piece, mine = call(
        down1,
        (gathered, inner, outer),
        [(13, 16, 128), (21, 16, 128)],
        [a1] * 12 + [(20, 32, 256), (20, 32, 128), (4, 8, 128)],
        "down1",
        40,
        [HBM] * 3,
    )
    near = apart(piece, 2)
    far = apart(piece, 4)
    pair_own = swapped(piece, 0)
    pair_near = swapped(near, 0)
    pair_far = swapped(far, 0)
    wide = lax.axis_size("wide")
    e2, sums = call(
        bottom,
        (mine, far, near, pair_own, pair_far, pair_near),
        [(ROOM, 16, 128), (wide // 4, 1, 128)],
        [(44, 16, 128)] * 9
        + [(22, 8, 128)] * 9
        + [(11, 8, 128)] * 9
        + [(40, 16, 128)] * 2
        + [(18, 8, 128)] * 2
        + [(5, 8, 128), (6, 16, 128), (8, 16, 128)],
        "bottom",
        1,
        None,
        [HBM, VMEM],
    )
    groups = [[i for i in range(wide) if (i // 2 + 2 * (i % 2)) % 4 == s] for s in range(4)]
    y_lo, y_hi, mobility, sav_vector, cotangent, sums = lax.optimization_barrier(
        (y_lo, y_hi, mobility, sav_vector, cotangent, sums)
    )
    every = lax.all_to_all(sums, "wide", 0, 0, axis_index_groups=groups)
    again = jnp.concatenate([y_lo, jnp.stack([mobility, sav_vector, cotangent]), y_hi], axis=2)
    out_s, out_c = call(
        up,
        (e2, gathered, inner, outer, again, x_inner, x_outer),
        [(16, 16, 256)] * 2,
        [a1] * 13
        + [a0] * 13
        + [(8, 32, 128), (8, 32, 256), (20, 48, 128), (20, 24, 128), (20, 24, 256), (8, 16, 128)],
        "up",
        46,
        [HBM] * 7,
    )
    return call(final, (every, out_s, out_c), [(16, 16, 256)], [(16, 16, 256)], "final", 4, None, [HBM])[0]


def solution(mesh):
    spec = P("wide", "narrow", None)
    return jax.shard_map(
        per_device, mesh=mesh, in_specs=(spec, spec, spec), out_specs=spec, check_vma=False
    )
```

```python
import functools

import jax
import jax.numpy as jnp
from jax import lax
from jax.experimental import pallas as pl
from jax.experimental.pallas import tpu as pltpu
from jax.sharding import PartitionSpec as P

f32 = jnp.float32
HALO = 4
LIMIT = 24
ROOM = 6144
C0, S0, W0, R0 = 22, 22, 20, 16
C1, S1, W1, R1 = 26, 26, 24, 8
C2, S2, W2, R2 = 42, 40, 38, 36
DAMPING = 0.8
BASE_TAU = 16.0
VMEM = pl.BlockSpec(memory_space=pltpu.VMEM)
HBM = pl.BlockSpec(memory_space=pltpu.HBM)


def half_tau(level):
    return 0.5 * BASE_TAU / 4.0**level


def iota(shape, dim):
    return lax.broadcasted_iota(jnp.int32, shape, dim)


def dot(x, matrix):
    matrix = matrix.astype(jnp.bfloat16)
    total = None
    for _ in range(3):
        part = x.astype(jnp.bfloat16)
        x = x - part.astype(f32)
        term = jnp.dot(part, matrix, preferred_element_type=f32)
        total = term if total is None else total + term
    return total


def rounded(x):
    return x.astype(jnp.bfloat16).astype(f32)


def ahead(x, axis):
    return pltpu.roll(x, x.shape[axis] - 1, axis)


def behind(x, axis):
    return pltpu.roll(x, 1, axis)


def at(i, n):
    return pl.ds(i, n) if n > 1 or not isinstance(i, int) else slice(i, i + 1)


def by_rows(lo, hi, n, fn, carry=None):
    count = (hi - lo) // n
    if count > 1:
        carry = lax.fori_loop(0, count, lambda t, c: fn(lo + t * n, n, c), carry)
    elif count == 1:
        carry = fn(lo, n, carry)
    rest = hi - lo - count * n
    if rest:
        carry = fn(lo + count * n, rest, carry)
    return carry


def coefficients(level, m, cx, cy, cz, dg, wt, lo, hi, n, y_len, z_len):
    tau = half_tau(level)
    cx[lo - 1] = rounded(tau * (m[lo - 1] + m[lo]))

    def body(i, n, carry):
        here = m[at(i, n)]
        shape = here.shape
        lane = lax.rem(iota(shape, 2), z_len)
        z_last = lane == z_len - 1
        z_first = lane == 0
        edge = rounded(tau * here)
        x_up = rounded(tau * (here + m[at(i + 1, n)]))
        cx[at(i, n)] = x_up
        y_up = rounded(tau * (here + ahead(here, 1)))
        if y_len is None:
            y_down = behind(y_up, 1)
            cy[at(i, n)] = y_up
        else:
            sub = iota(shape, 1)
            inner = jnp.where(sub >= y_len - 1, 0.0, y_up)
            y_up = jnp.where(sub == y_len - 1, edge, y_up)
            y_down = jnp.where(sub == 0, edge, behind(inner, 1))
            cy[at(i, n)] = inner
        inner = jnp.where(z_last, 0.0, rounded(tau * (here + ahead(here, 2))))
        cz[at(i, n)] = inner
        z_up = jnp.where(z_last, edge, inner)
        z_down = jnp.where(z_first, edge, behind(inner, 2))
        diagonal = 1.0 + x_up + cx[at(i - 1, n)] + y_up + y_down + z_up + z_down
        if dg is not None:
            dg[at(i, n)] = diagonal
        wt[at(i, n)] = jnp.where(here > 0.0, DAMPING / diagonal, 0.0)
        return carry

    by_rows(lo, hi, n, body, 0)


def coupled(i, n, v, cx, cy, cz):
    here = v[at(i, n)]
    up = cy[at(i, n)]
    side = cz[at(i, n)]
    total = cx[at(i, n)] * v[at(i + 1, n)] + cx[at(i - 1, n)] * v[at(i - 1, n)]
    total = total + (up * ahead(here, 1) + behind(up * here, 1))
    return total + (side * ahead(here, 2) + behind(side * here, 2))


def residual(i, n, r, v, cx, cy, cz, dg):
    return r - dg[at(i, n)] * v[at(i, n)] + coupled(i, n, v, cx, cy, cz)


def relaxed(i, n, r, v, wt, cx, cy, cz, *_):
    return (1.0 - DAMPING) * v[at(i, n)] + wt[at(i, n)] * (r[at(i, n)] + coupled(i, n, v, cx, cy, cz))


def start(lo, hi, n, source, out, wt):
    def body(i, n, carry):
        for s, o in zip(source, out):
            o[at(i, n)] = wt[at(i, n)] * s[at(i, n)]
        return carry

    by_rows(lo, hi, n, body, 0)


def sweep(lo, hi, n, source, v, out, coefs, wt):
    def body(i, n, carry):
        for s, a, o in zip(source, v, out):
            o[at(i, n)] = relaxed(i, n, s, a, wt, *coefs)
        return carry

    by_rows(lo, hi, n, body, 0)


def pairs(x):
    x = x.reshape(x.shape[0] // 2, 2, *x.shape[1:])
    return x[:, 0] + x[:, 1]


def doubled(x):
    x = jnp.broadcast_to(x[:, None], (x.shape[0], 2, *x.shape[1:]))
    return x.reshape(x.shape[0] * 2, *x.shape[2:])


def flat_dot(x, matrix):
    n = x.shape[0] * x.shape[1]
    return dot(x.reshape(n, x.shape[2]), matrix).reshape(x.shape[0], x.shape[1], matrix.shape[1])


def fold_y(ref, k, n, first, count):
    return ref[k : k + n, pl.ds(first, count, stride=2), :] + ref[k : k + n, pl.ds(first + 1, count, stride=2), :]


def coarse_z(z_in, lanes_in, z_out, lanes_out, fields):
    src = iota((lanes_in, lanes_out), 0)
    dst = iota((lanes_in, lanes_out), 1)
    target = lax.div(src, z_in) * z_out + lax.div(lax.rem(src, z_in), 2)
    return jnp.where((target == dst) & (src < fields * z_in), 0.125, 0.0).astype(f32)


def fine_z(z_in, lanes_in, z_out, lanes_out, fields):
    src = iota((lanes_in, lanes_out), 0)
    dst = iota((lanes_in, lanes_out), 1)
    wanted = lax.div(dst, z_out) * z_in + lax.div(lax.rem(dst, z_out), 2)
    return jnp.where((wanted == src) & (dst < fields * z_out), 1.0, 0.0).astype(f32)


def products(i, n, s, c, us, uc, coefs, sums):
    num, den = sums
    v_s, v_c = us[at(i, n)], uc[at(i, n)]
    r_s, r_c = s[at(i, n)], c[at(i, n)]
    res_s = residual(i, n, r_s, us, *coefs)
    res_c = residual(i, n, r_c, uc, *coefs)
    num = num + jnp.sum(v_s * r_c + res_s * v_c, axis=0)
    den = den + jnp.sum(v_s * r_s + res_s * v_s, axis=0)
    return res_s, res_c, (num, den)


def fetch(sources, targets, sems):
    copies = [pltpu.make_async_copy(a, b, sems.at[k]) for k, (a, b) in enumerate(zip(sources, targets))]
    for copy in copies:
        copy.start()
    return copies


def wait(copies):
    for copy in copies:
        copy.wait()


def sides(low, high):
    even = lax.rem(lax.axis_index("wide"), 2) == 0
    return jnp.where(even, high, low), jnp.where(even, low, high)


def fetch0(own, inner, outer, fields, sems):
    sources, targets = [], []
    for index, ref in enumerate(fields):
        n = 3 if index else 4
        first = 4 + 3 * (index - 1) if index else 0
        inner_at, outer_at = sides(4 - n, 20)
        edges = ((inner, inner_at), (outer, outer_at))
        sources += [part.at[pl.ds(first, n)] for part, _ in edges]
        targets += [ref.at[pl.ds(lo, n)] for _, lo in edges]
        if own is not None:
            sources.append(own.at[index])
            targets.append(ref.at[pl.ds(4, 16)])
    return fetch(sources, targets, sems)


def fetch1(own, inner, outer, fields, sems):
    sources, targets = [], []
    for index, ref in fields:
        n = 8 if index == 2 else 6
        inner_at, _ = sides(2, 18)
        _, outer_at = sides(10 - n, 18)
        for source, first, lo, rows in (
            (own, 8 * index, 10, 8),
            (inner, 8 * index, inner_at, 8),
            (outer, 6 * index, outer_at, n),
        ):
            for j in range(4):
                sources.append(source.at[j, pl.ds(first, rows)])
                targets.append(ref.at[pl.ds(lo, rows), pl.ds(8 * j, 8), :])
    return fetch(sources, targets, sems)


def down0(own, outer, inner, out, vs, vc, cx, cy, cz, dg, wt, ss, cc, m, us, uc, pair, thin, sems):
    copies = fetch0(None, inner, outer, (m, ss, cc), sems)
    for index, ref in enumerate((m, ss, cc)):
        ref[4:20] = own[index]
    wait(copies[:2])
    coefficients(0, m, cx, cy, cz, dg, wt, 1, 23, C0, None, 256)
    coefs = (cx, cy, cz, dg)
    wait(copies[2:])
    start(1, 23, S0, (ss, cc), (us, uc), wt)
    sweep(2, 22, W0, (ss, cc), (us, uc), (vs, vc), coefs, wt)

    def rest(i, n, sums):
        res_s, res_c, sums = products(i, n, ss, cc, vs, vc, coefs, sums)
        k = lax.div(i - 4, 2)
        pair[at(k, n // 2)] = pairs(res_s)
        pair[at(k + 8, n // 2)] = pairs(res_c)
        pair[at(k + 16, n // 2)] = pairs(m[at(i, n)])
        return sums

    zero = jnp.zeros((24, 256), f32)
    num, den = by_rows(4, 20, R0, rest, (zero, zero))
    thin[...] = flat_dot(pair[...], coarse_z(256, 256, 128, 128, 1))
    value = fold_y(thin, 0, 24, 4, 8)
    sub = iota((24, 256), 0)
    inside = (sub >= 4) & (sub < 20)
    num = jnp.sum(jnp.where(inside, num, 0.0))
    den = jnp.sum(jnp.where(inside, den, 0.0))
    lane = iota((8, 128), 1)
    both = jnp.where(lane == 0, num, jnp.where(lane == 1, den, 0.0))
    for j in range(4):
        out[j, 0:24] = value
        out[j, 24] = both


def down1(
    own, outer, inner, piece, mine,
    vs, vc, cx, cy, cz, dg, wt, ss, cc, m, us, uc, pair, thin, parts, sems,
):
    copies = fetch1(own, inner, outer, ((2, m), (0, ss), (1, cc)), sems)
    partial = fetch([own.at[j, 24] for j in range(4)], [parts.at[j] for j in range(4)], sems.at[pl.ds(36, 4)])
    wait(copies[:12])
    coefficients(1, m, cx, cy, cz, dg, wt, 4, 24, C1, 32, 128)
    coefs = (cx, cy, cz, dg)
    wait(copies[12:])
    wait(partial)
    start(4, 24, S1, (ss, cc), (us, uc), wt)
    sweep(5, 23, W1, (ss, cc), (us, uc), (vs, vc), coefs, wt)

    def rest(i, n, sums):
        res_s, res_c, sums = products(i, n, ss, cc, vs, vc, coefs, sums)
        k = (i - 6) // 2
        pair[at(k, n // 2), :, 0:128] = pairs(res_s)
        pair[at(k, n // 2), :, 128:256] = pairs(res_c)
        return sums

    zero = jnp.zeros((32, 128), f32)
    rest(6, 4, (zero, zero))
    num, den = rest(10, 8, (zero, zero))
    rest(18, 4, (zero, zero))
    both = pairs(m[2:26])
    pair[8:20, :, 0:128] = both
    pair[8:20, :, 128:256] = both
    thin[...] = flat_dot(pair[...], coarse_z(128, 256, 64, 128, 2))
    mid = fold_y(thin, 0, 8, 0, 16)
    mob = fold_y(thin, 8, 12, 0, 16)
    even = lax.rem(lax.axis_index("wide"), 2) == 0
    mine[0:8] = mid
    mine[8:20] = mob
    piece[0:8] = mid
    left = iota((4, 16, 128), 2) < 64
    piece[8:12] = jnp.where(
        left, jnp.where(even, mob[0:4], mob[4:8]), jnp.where(even, mob[4:8], mob[8:12])
    )
    lane = iota((8, 128), 1)
    num = jnp.sum(num) * 8.0
    den = jnp.sum(den) * 8.0
    finer = parts[0] + parts[1] + parts[2] + parts[3]
    total = finer + jnp.where(lane == 0, num, jnp.where(lane == 1, den, 0.0))
    for ref, row in ((piece, 12), (mine, 20)):
        ref[row] = jnp.concatenate([total, total], axis=0)


def bottom(
    mine, far, near, pair_own, pair_far, pair_near, e2_out, sums,
    m2, r2, u2, v2, cx2, cy2, cz2, dg2, wt2,
    m3, r3, u3, v3, cx3, cy3, cz3, dg3, wt3,
    m4, r4, u4, v4, cx4, cy4, cz4, dg4, wt4,
    pair2, thin2, pair3, thin3, wide3, wide2, e2, sems,
):
    left = iota((4, 16, 128), 2) < 64
    place = lax.axis_index("wide")
    size = lax.axis_size("wide")

    even = lax.rem(place, 2) == 0

    def choose(a, b):
        return jnp.where(even, a, b)

    def held(distance, value):
        return jnp.where((place + distance >= 0) & (place + distance < size), value, 0.0)

    def unpack(ref, distance):
        packed = held(distance, ref[8:12])
        other = pltpu.roll(packed, 64, 2)
        return held(distance, ref[0:8]), jnp.where(left, packed, other), jnp.where(left, other, packed)

    r2[18:26] = mine[0:8]
    m2[16:28] = mine[8:20]
    for ref, distance, r_at, m_at in (
        (near, choose(-2, 2), choose(10, 26), choose(8, 28)),
        (far, choose(-4, 4), choose(2, 34), choose(0, 36)),
        (pair_near, choose(3, -3), choose(30, 6), choose(32, 4)),
    ):
        cells, m_low, m_high = unpack(ref, distance)
        r2[pl.ds(r_at, 8)] = cells
        m2[pl.ds(m_at, 4)] = m_low
        m2[pl.ds(m_at + 4, 4)] = m_high
    cells, m_low, m_high = unpack(pair_own, 0)
    r2[pl.ds(choose(26, 14), 4)] = choose(cells[4:8], cells[0:4])
    m2[pl.ds(choose(28, 12), 4)] = choose(m_high, m_low)
    cells, m_low, m_high = unpack(pair_far, choose(5, -5))
    r2[pl.ds(choose(38, 2), 4)] = choose(cells[0:4], cells[4:8])
    m2[pl.ds(choose(40, 0), 4)] = choose(m_low, m_high)

    lo = jnp.where(even, jnp.where(place == 2, -2, 0), jnp.where(place == 3, -3, -2))
    hi = jnp.where(place == size - 4, 3, 2)

    def both_products(r, v, res, z_len, rows):
        num = v * pltpu.roll(r, 128 - z_len, 2)
        den = v * r
        if res is not None:
            num = num + res * pltpu.roll(v, 128 - z_len, 2)
            den = den + res * v
        device = lax.div(iota(v.shape, 0), rows) - 3
        mask = (iota(v.shape, 2) < z_len) & (device >= lo) & (device <= hi)
        num = jnp.sum(jnp.where(mask, num, 0.0), axis=0)
        den = jnp.sum(jnp.where(mask, den, 0.0), axis=0)
        return num, den

    c2 = (cx2, cy2, cz2, dg2)
    c3 = (cx3, cy3, cz3, dg3)
    c4 = (cx4, cy4, cz4, dg4)
    coefficients(2, m2, *c2, wt2, 1, 43, C2, 16, 64)
    start(2, 42, S2, (r2,), (u2,), wt2)
    sweep(3, 41, W2, (r2,), (u2,), (v2,), c2, wt2)

    res = residual(4, 36, r2[4:40], v2, *c2)
    pair2[0:18] = pairs(res)
    kept = slice(8, 36)
    num2, den2 = both_products(r2[kept], v2[kept], res[4:32], 64, 4)
    pair2[18:40] = pairs(m2[...])
    thin2[...] = flat_dot(pair2[...], coarse_z(64, 128, 32, 128, 2))
    r3[2:20] = fold_y(thin2, 0, 18, 0, 8)
    m3[...] = fold_y(thin2, 18, 22, 0, 8)

    coefficients(3, m3, *c3, wt3, 1, 21, 10, 8, 32)
    start(2, 20, 18, (r3,), (u3,), wt3)
    sweep(3, 19, 16, (r3,), (u3,), (v3,), c3, wt3)
    res = residual(4, 14, r3[4:18], v3, *c3)
    kept = slice(4, 18)
    num3, den3 = both_products(r3[kept], v3[kept], res, 32, 2)
    pair3[0:7] = pairs(res)
    pair3[7:18] = pairs(m3[...])
    thin3[...] = flat_dot(pair3[...], coarse_z(32, 128, 16, 128, 2))
    m4[...] = jnp.zeros((11, 8, 128), f32)
    r4[...] = jnp.zeros((11, 8, 128), f32)
    r4[2:9, 0:4, :] = fold_y(thin3, 0, 7, 0, 4)
    m4[:, 0:4, :] = fold_y(thin3, 7, 11, 0, 4)

    coefficients(4, m4, *c4, wt4, 1, 10, 9, 4, 16)
    u4[1] = jnp.zeros((8, 128), f32)
    u4[9] = jnp.zeros((8, 128), f32)
    start(2, 9, 7, (r4,), (u4,), wt4)
    sweep(2, 9, 7, (r4,), (u4,), (v4,), c4, wt4)
    wide3[:, pl.ds(0, 4, stride=2), :] = v4[3:8, 0:4, :]
    wide3[:, pl.ds(1, 4, stride=2), :] = v4[3:8, 0:4, :]
    v3[6:16] = v3[6:16] + doubled(flat_dot(wide3[...], fine_z(16, 128, 32, 128, 2)))
    sweep(7, 15, 8, (r3,), (v3,), (u3,), c3, wt3)
    sweep(8, 14, 6, (r3,), (u3,), (v3,), c3, wt3)
    wide2[:, pl.ds(0, 8, stride=2), :] = v3[8:14]
    wide2[:, pl.ds(1, 8, stride=2), :] = v3[8:14]
    v2[16:28] = v2[16:28] + doubled(flat_dot(wide2[...], fine_z(32, 128, 64, 128, 2)))
    sweep(17, 27, 10, (r2,), (v2,), (u2,), c2, wt2)
    e2[...] = relaxed(18, 8, r2, u2, wt2, *c2)
    copies = fetch([e2], [e2_out.at[pl.ds(0, 8)]], sems)
    kept = slice(2, 9)
    num4, den4 = both_products(r4[kept], v4[kept], None, 16, 1)
    num = 64.0 * jnp.sum(num2) + 512.0 * jnp.sum(num3) + 4096.0 * jnp.sum(num4)
    den = 64.0 * jnp.sum(den2) + 512.0 * jnp.sum(den3) + 4096.0 * jnp.sum(den4)
    lane = iota((8, 128), 1)
    finer = mine[20, 0:8] + near[12, 0:8] + pair_own[12, 0:8] + pair_near[12, 0:8]
    total = finer + jnp.where(lane == 0, num, jnp.where(lane == 1, den, 0.0))
    sums[...] = jnp.broadcast_to(total[0:1].reshape(1, 1, 128), sums.shape)
    wait(copies)


def up(
    e2_in, own1, inner1, outer1, own0, inner0, outer0, out_s, out_c,
    vs1, vc1, cx1, cy1, cz1, wt1, ss1, cc1, m1, as1, ac1, bs1, bc1,
    vs0, vc0, cx0, cy0, cz0, wt0, ss0, cc0, m0, as0, ac0, bs0, bc0,
    wide, add, block, thick, full, e2, sems,
):
    copies1 = fetch1(own1, inner1, outer1, ((2, m1), (0, ss1), (1, cc1)), sems)
    copies0 = fetch0(own0, inner0, outer0, (m0, ss0, cc0), sems.at[pl.ds(36, 9)])
    copies2 = fetch([e2_in.at[pl.ds(0, 8)]], [e2], sems.at[pl.ds(45, 1)])
    c1 = (cx1, cy1, cz1)
    c0 = (cx0, cy0, cz0)
    wait(copies1)
    coefficients(1, m1, cx1, cy1, cz1, None, wt1, 5, 23, C1, 32, 128)
    start(5, 23, S1, (ss1, cc1), (as1, ac1), wt1)
    sweep(6, 22, W1, (ss1, cc1), (as1, ac1), (vs1, vc1), c1, wt1)
    wait(copies0)
    coefficients(0, m0, cx0, cy0, cz0, None, wt0, 1, 23, C0, None, 256)
    start(1, 23, S0, (ss0, cc0), (as0, ac0), wt0)
    sweep(2, 22, W0, (ss0, cc0), (as0, ac0), (vs0, vc0), c0, wt0)
    wait(copies2)
    wide[:, pl.ds(0, 16, stride=2), :] = e2[...]
    wide[:, pl.ds(1, 16, stride=2), :] = e2[...]
    add[...] = flat_dot(wide[...], fine_z(64, 128, 128, 256, 2))

    def correct1(i, n, carry):
        k = lax.div(i - 6, 2)
        both = add[at(k, n // 2)]
        as1[at(i, n)] = vs1[at(i, n)] + doubled(both[:, :, 0:128])
        ac1[at(i, n)] = vc1[at(i, n)] + doubled(both[:, :, 128:256])
        return carry

    by_rows(6, 22, R1, correct1, 0)
    sweep(8, 20, W1, (ss1, cc1), (as1, ac1), (bs1, bc1), c1, wt1)
    place = lax.axis_index("narrow")
    block[:, 0:8, :] = jnp.zeros((20, 8, 128), f32)
    block[:, 40:48, :] = jnp.zeros((20, 8, 128), f32)

    def last1(i, n, carry):
        for index, (r, v) in enumerate(((ss1, bs1), (cc1, bc1))):
            value = relaxed(i, n, r, v, wt1, *c1)
            block[at(index * 10 + i - 9, n), 8:40, :] = value
        return carry

    by_rows(9, 19, 5, last1, 0)
    value = block[:, pl.ds(pl.multiple_of(8 * place, 8), 24), :][:, 6:18, :]
    thick[:, pl.ds(0, 12, stride=2), :] = value
    thick[:, pl.ds(1, 12, stride=2), :] = value
    full[...] = flat_dot(thick[...], fine_z(128, 128, 256, 256, 1))

    def correct0(i, n, carry):
        k = lax.div(i - 2, 2)
        as0[at(i, n)] = vs0[at(i, n)] + doubled(full[at(k, n // 2)])
        ac0[at(i, n)] = vc0[at(i, n)] + doubled(full[at(10 + k, n // 2)])
        return carry

    by_rows(2, 22, R0, correct0, 0)
    sweep(3, 21, W0, (ss0, cc0), (as0, ac0), (bs0, bc0), c0, wt0)

    def last0(i, n, carry):
        for r, v, o in ((ss0, bs0, out_s), (cc0, bc0, out_c)):
            o[at(i - 4, n)] = relaxed(i, n, r, v, wt0, *c0)[:, 4:20, :]
        return carry

    by_rows(4, 20, W0, last0, 0)


def final(every, out_s, out_c, out, held, sems):
    total = jnp.sum(every[...], axis=0)
    lane = iota((1, 128), 1)
    num = jnp.sum(jnp.where(lane == 0, total, 0.0), axis=1, keepdims=True)
    den = jnp.sum(jnp.where(lane == 1, total, 0.0), axis=1, keepdims=True)
    ratio = (num / (1.0 + den))[0, 0]
    copies = []
    for k in range(4):
        rows = pl.ds(4 * k, 4)
        held[rows] = out_c[rows] - ratio * out_s[rows]
        copies += fetch([held.at[rows]], [out.at[rows]], sems.at[pl.ds(k, 1)])
    wait(copies)


def call(kernel, ins, outs, scratch, name, sems=0, specs=None, out_specs=None):
    scratch = [pltpu.VMEM(s, f32) for s in scratch]
    if sems:
        scratch.append(pltpu.SemaphoreType.DMA((sems,)))
    return pl.pallas_call(
        kernel,
        out_shape=[jax.ShapeDtypeStruct(s, f32) for s in outs],
        in_specs=specs or [VMEM] * len(ins),
        out_specs=out_specs or [VMEM] * len(outs),
        scratch_shapes=scratch,
        compiler_params=pltpu.CompilerParams(vmem_limit_bytes=LIMIT * 2**20),
        name=name,
    )(*ins)


def shifted(value, axis, by):
    size = lax.axis_size(axis)
    return lax.ppermute(value, axis, [(i, i + by) for i in range(size) if 0 <= i + by < size])


def apart(value, by):
    size = lax.axis_size("wide")
    return lax.ppermute(value, "wide", [(i, (i + by * (1 - 2 * (i % 2))) % size) for i in range(size)])


def swapped(value, first):
    pairs = [(i, i + 1) for i in range(first, lax.axis_size("wide") - 1, 2)]
    return lax.ppermute(value, "wide", pairs + [(b, a) for a, b in pairs])


def per_device(mobility, sav_vector, cotangent):
    whole = jnp.stack([mobility, sav_vector, cotangent])
    y_lo = shifted(whole[:, :, -HALO:], "narrow", 1)
    y_hi = shifted(whole[:, :, :HALO], "narrow", -1)
    own = jnp.concatenate([y_lo, whole, y_hi], axis=2)
    odd = lax.rem(lax.axis_index("wide"), 2)

    def edge(at_end):
        return jnp.concatenate(
            [
                lax.dynamic_slice_in_dim(own[index], at_end * (16 - n), n, axis=0)
                for index, n in enumerate((HALO, HALO - 1, HALO - 1))
            ]
        )

    x_inner = swapped(edge(1 - odd), 0)
    x_outer = swapped(edge(odd), 1)
    a0 = (24, 24, 256)
    (chunk,) = call(
        down0,
        (own, x_outer, x_inner),
        [(4, 25, 8, 128)],
        [a0] * 13 + [(24, 24, 128)],
        "down0",
        6,
        [VMEM] + [HBM] * 2,
    )
    gathered = lax.all_to_all(chunk, "narrow", 0, 0)
    edges = [lax.dynamic_slice_in_dim(gathered, 8 * index + 2 * odd, 6, axis=1) for index in range(2)]
    outer = swapped(jnp.concatenate([*edges, gathered[:, 16:24]], axis=1), 1)
    inner = swapped(gathered, 0)
    a1 = (28, 32, 128)
    piece, mine = call(
        down1,
        (gathered, outer, inner),
        [(13, 16, 128), (21, 16, 128)],
        [a1] * 12 + [(20, 32, 256), (20, 32, 128), (4, 8, 128)],
        "down1",
        40,
        [HBM] * 3,
    )
    near = apart(piece, 2)
    far = apart(piece, 4)
    pair_own = swapped(piece, 0)
    pair_near = swapped(near, 0)
    pair_far = swapped(far, 0)
    wide = lax.axis_size("wide")
    e2, sums = call(
        bottom,
        (mine, far, near, pair_own, pair_far, pair_near),
        [(ROOM, 16, 128), (wide // 4, 1, 128)],
        [(44, 16, 128)] * 9
        + [(22, 8, 128)] * 9
        + [(11, 8, 128)] * 9
        + [(40, 16, 128)] * 2
        + [(18, 8, 128)] * 2
        + [(5, 8, 128), (6, 16, 128), (8, 16, 128)],
        "bottom",
        1,
        None,
        [HBM, VMEM],
    )
    groups = [[i for i in range(wide) if (i // 2 + 2 * (i % 2)) % 4 == s] for s in range(4)]
    y_lo, y_hi, mobility, sav_vector, cotangent, sums = lax.optimization_barrier(
        (y_lo, y_hi, mobility, sav_vector, cotangent, sums)
    )
    every = lax.all_to_all(sums, "wide", 0, 0, axis_index_groups=groups)
    again = jnp.concatenate([y_lo, jnp.stack([mobility, sav_vector, cotangent]), y_hi], axis=2)
    out_s, out_c = call(
        up,
        (e2, gathered, inner, outer, again, x_inner, x_outer),
        [(16, 16, 256)] * 2,
        [a1] * 13
        + [a0] * 13
        + [(8, 32, 128), (8, 32, 256), (20, 48, 128), (20, 24, 128), (20, 24, 256), (8, 16, 128)],
        "up",
        46,
        [HBM] * 7,
    )
    return call(final, (every, out_s, out_c), [(16, 16, 256)], [(16, 16, 256)], "final", 4, None, [HBM])[0]


def solution(mesh):
    spec = P("wide", "narrow", None)
    return jax.shard_map(
        per_device, mesh=mesh, in_specs=(spec, spec, spec), out_specs=spec, check_vma=False
    )
```
